256 devices in a mesh: blk: 4 (over z_lo), sample: 64 (over y, x, z_hi, core).
Axes of the slice: x: 4, y: 4, z: 8 (z_hi: 2, z_lo: 4; z = z_hi * 4 + z_lo), core: 2. Of those that a mesh axis runs over, the one named last changes fastest.
Arguments:
- labels: bfloat16 [64, 4096, 512], P('sample', 'blk'), may hold values from -6 to 6
- basis: bfloat16 [64, 4096, 1024], P('sample', 'blk'), may hold values from -0.01171875 to 0.01171875
- gains: float32 [1024], replicated, may hold values from 2 to 32
- tiles: bfloat16 [64, 16, 4, 256, 256], P('sample', 'blk'), may hold values from 0 to 0.0029296875
- tile_cols: int32 [64, 16, 4], P('sample', 'blk'), may hold values from 0 to 15
- tile_valid: int32 [64, 16, 4], P('sample', 'blk'), may hold values 0 or 1
Outputs:
- solution: float32 [64, 4096, 512], P('sample', 'blk')
- residual: float32 [64, 4096, 512], P('sample', 'blk')
The draws below stay inside these ranges and needn't reach their ends.
All inputs are finite; a program needn't handle non-finite values. No bound on the sum of `tile_valid` on one device may be relied on, other than what follows from the above.
Results may differ from the reference program's by a relative error of at most 0.0022.
Values may be sent and summed in bfloat16 or wider, within the bound.
No kernel may reach another device: no remote copies, remote signals or barrier semaphores. Data moves between devices by JAX's collectives and lax.ppermute only.
A program may use at most 64 MiB of HBM per device.

```python
import math
import jax
import jax.numpy as jnp
from jax import lax

K = 512
R = 1024
TILE = 256
TPR = 4
ITERS = 1
CLUSTER_ROWS = 4096
CLUSTERS = 64
ROW_BLOCKS = 16
NODES = 262144


def draw_labels(key, part):
    key = jax.random.fold_in(key, 11)
    key_noise, key_offset = jax.random.split(key)
    noise = 0.6 * jnp.clip(jax.random.normal(key_noise, (CLUSTERS, CLUSTER_ROWS, K), jnp.float32), -4.0, 4.0)
    offset = jnp.clip(jax.random.normal(key_offset, (CLUSTERS, ROW_BLOCKS, 1, K), jnp.float32), -3.0, 3.0)
    spread = jnp.broadcast_to(offset, (CLUSTERS, ROW_BLOCKS, TILE, K)).reshape(CLUSTERS, CLUSTER_ROWS, K)
    return (noise + spread).astype(jnp.bfloat16)


def touch_ends(array, rng, least, largest):
    spot = [jax.random.randint(jax.random.fold_in(rng, axis), (), 0, length) for axis, length in enumerate(array.shape)]
    longest = array.shape.index(max(array.shape))
    neighbour = spot[:longest] + [(spot[longest] + 1) % array.shape[longest]] + spot[longest + 1:]
    return array.at[tuple(spot)].set(least).at[tuple(neighbour)].set(largest)


def steps_of(rng, shape, cuts, smallest, largest):
    factor_of = 1.0
    for dim, parts in cuts:
        steps = jax.random.uniform(jax.random.fold_in(jax.random.fold_in(rng, 6), dim), (parts,), jnp.float32, smallest / len(cuts), largest / len(cuts))
        factor_of = factor_of * jnp.repeat(jnp.exp(steps), shape[dim] // parts).reshape((-1,) + (1,) * (len(shape) - 1 - dim))
    return factor_of


def normal_values(key, extent, scale, reach, cuts=(), kind=jnp.bfloat16):
    values = jax.random.normal(key, extent, jnp.float32) * scale
    if len(cuts) > 0:
        values = steps_of(key, extent, cuts, -0.22, 0.18) * values
    return jnp.clip(values, min=-reach, max=reach).astype(kind)


def setup_inputs(seed: int = 0) -> dict:
    seeds = jax.random.split(jax.random.key(seed), 7)
    return {
        "labels": draw_labels(jax.random.fold_in(seeds[6], 71), 0),
        "basis": normal_values(seeds[1], (CLUSTERS, CLUSTER_ROWS, R), NODES ** -0.5, 0.01171875, ((0, 64), (1, 4))),
        "gains": jnp.clip(jnp.exp(jax.random.uniform(seeds[2], (R,), jnp.float32, math.log(2.0), math.log(32.0))), 2.0, 32.0),
        "tiles": jnp.clip(0.0029296875 * jax.random.uniform(seeds[3], (CLUSTERS, ROW_BLOCKS, TPR, TILE, TILE), jnp.float32) ** steps_of(seeds[3], (CLUSTERS, ROW_BLOCKS, TPR, TILE, TILE), ((0, 64), (1, 4)), -0.2, 0.2), 0.0, 0.0029296875).astype(jnp.bfloat16),
        "tile_cols": touch_ends(jax.random.randint(seeds[4], (CLUSTERS, ROW_BLOCKS, TPR), 0, ROW_BLOCKS), jax.random.fold_in(seeds[4], 1), 0, ROW_BLOCKS - 1).astype(jnp.int32),
        "tile_valid": touch_ends((jax.random.randint(seeds[5], (CLUSTERS, ROW_BLOCKS, TPR), 0, 4) < 3).astype(jnp.int32), jax.random.fold_in(seeds[5], 1), 0, 1),
    }


def cluster_degree(pack):
    tiles_c, cols_c, valid_c = pack
    validf = valid_c.astype(jnp.float32)
    tilesf = tiles_c.astype(jnp.float32)
    row_part = jnp.sum(tilesf, axis=3)
    row_total = jnp.sum(row_part * validf[:, :, None], axis=1).reshape(-1)
    col_part = jnp.sum(tilesf, axis=2)
    onehot = (cols_c[:, :, None] == jnp.arange(ROW_BLOCKS, dtype=jnp.int32)[None, None, :]).astype(jnp.float32) * validf[:, :, None]
    col_total = jnp.einsum('btc,bti->ci', onehot, col_part, precision=lax.Precision.HIGHEST).reshape(-1)
    return 0.5 * (row_total + col_total)


def cluster_apply(pack):
    vector, tiles_c, cols_c, valid_c, degree = pack
    blocks = vector.astype(jnp.bfloat16).reshape(ROW_BLOCKS, TILE, K)
    chosen = blocks[cols_c]
    product = jnp.einsum('btij,btjk->btik', tiles_c.astype(jnp.float32), chosen.astype(jnp.float32))
    weighted = jnp.sum(product * valid_c.astype(jnp.float32)[:, :, None, None], axis=1).reshape(CLUSTER_ROWS, K)
    return vector + 0.5 * (degree[:, None] * vector - weighted)


def reference(labels, basis, gains, tiles, tile_cols, tile_valid):
    degree = lax.map(cluster_degree, (tiles, tile_cols, tile_valid))

    def apply_a(vector):
        return lax.map(cluster_apply, (vector, tiles, tile_cols, tile_valid, degree))

    def precondition(vector):
        rounded = vector.astype(jnp.bfloat16)

        def accumulate(total, pack):
            return total + jnp.dot(pack[0].T, pack[1], preferred_element_type=jnp.float32), None

        projection, unused = lax.scan(accumulate, jnp.zeros((R, K), jnp.float32), (basis, rounded))
        coeffs = (gains[:, None] * projection).astype(jnp.bfloat16)
        spread = lax.map(lambda rows: jnp.dot(rows, coeffs, preferred_element_type=jnp.float32), basis)
        return vector + spread

    def col_dot(first, second):
        return jnp.sum(first * second, axis=(0, 1))

    residual = labels.astype(jnp.float32)
    solution = jnp.zeros_like(residual)
    search = precondition(residual)
    norm_now = col_dot(residual, search)
    for step in range(ITERS):
        image = apply_a(search)
        step_size = norm_now / col_dot(search, image)
        solution = solution + step_size * search
        residual = residual - step_size * image
        if step + 1 < ITERS:
            precond = precondition(residual)
            norm_next = col_dot(residual, precond)
            search = precond + (norm_next / norm_now) * search
            norm_now = norm_next
    return solution, residual
```

```python
import jax
import jax.numpy as jnp
from jax import lax
from jax.experimental import pallas as pl
from jax.experimental.pallas import tpu as pltpu
from jax.sharding import Mesh, PartitionSpec as P

F32 = jnp.float32
BF16 = jnp.bfloat16
FINE = ("blk", "y", "x", "zh", "core")
SAMPLE = ("y", "x", "zh", "core")
VMEM_LIMIT = 48 * 1024 * 1024


def shift(value, axis, by):
    size = lax.axis_size(axis)
    return lax.ppermute(value, axis, [(i, (i + by) % size) for i in range(size)])


def along_line(value, by, skip):
    size = lax.axis_size("blk")
    if by > 0:
        pairs = [(i, i + 1) for i in range(skip, size - 1)]
    else:
        pairs = [(i, i - 1) for i in range(1, size - skip)]
    return lax.ppermute(value, "blk", pairs)


def reduce_scatter(value, axis):
    size = lax.axis_size(axis)
    me = lax.axis_index(axis)
    rows = value.shape[0] // size
    parts = [
        lax.dynamic_slice_in_dim(value, ((me + k) % size) * rows, rows) for k in range(size)
    ]
    got = [shift(parts[k], axis, k) for k in range(1, size)]
    total = parts[0]
    for part in got:
        total = total + part
    return total


def all_sum(value, axis):
    total = value
    for part in [shift(value, axis, k) for k in range(1, lax.axis_size(axis))]:
        total = total + part
    return total


def degree_parts_kernel(cols, valid, tiles, rows_out, cols_out):
    step = pl.program_id(0)
    slots = tiles.shape[0]

    @pl.when(step == 0)
    def _():
        cols_out[...] = jnp.zeros_like(cols_out)

    total = jnp.zeros(tiles.shape[1:], F32)
    for t in range(slots):
        at = step * slots + t
        tile = tiles[t].astype(F32) * valid[at].astype(F32)
        total = total + tile
        cols_out[pl.ds(cols[at], 1), :] += jnp.sum(tile, axis=0, keepdims=True)
    rows_out[...] = jnp.sum(total, axis=1, keepdims=True)


def degree_parts(tiles, cols, valid, col_blocks, slots):
    count, size, _ = tiles.shape
    steps = count // slots
    return pl.pallas_call(
        degree_parts_kernel,
        grid_spec=pltpu.PrefetchScalarGridSpec(
            num_scalar_prefetch=2,
            grid=(steps,),
            in_specs=[pl.BlockSpec((slots, size, size), lambda i, c, v: (i, 0, 0))],
            out_specs=[
                pl.BlockSpec((size, 1), lambda i, c, v: (i, 0)),
                pl.BlockSpec((col_blocks, size), lambda i, c, v: (0, 0)),
            ],
        ),
        out_shape=[
            jax.ShapeDtypeStruct((steps * size, 1), F32),
            jax.ShapeDtypeStruct((col_blocks, size), F32),
        ],
        cost_estimate=pl.CostEstimate(
            flops=4 * tiles.size, bytes_accessed=2 * tiles.size, transcendentals=0
        ),
        name="degree_parts",
    )(cols, valid, tiles)


def spread_kernel(place, labels, basis, mine, theirs, search, rounded, dots, coeffs):
    step = pl.program_id(0)
    rows = mine.shape[1]
    parts = mine.shape[0]

    @pl.when(step == 0)
    def _():
        dots[...] = jnp.zeros_like(dots)
        for k in range(parts):
            at = place[0] * parts + lax.rem(place[1] + parts - k, parts)
            coeffs[pl.ds(pl.multiple_of(at * rows, rows), rows), :] = mine[k]
            at = (1 - place[0]) * parts + lax.rem(place[1] + parts - k, parts)
            coeffs[pl.ds(pl.multiple_of(at * rows, rows), rows), :] = theirs[k]

    residual = labels[...].astype(F32)
    value = residual + jnp.dot(basis[...], coeffs[...], preferred_element_type=F32)
    search[...] = value
    rounded[...] = value.astype(BF16)
    dots[...] += jnp.sum(residual * value, axis=0, keepdims=True)


def spread(place, labels, basis, mine, theirs):
    rows, classes = labels.shape
    rank = basis.shape[1]
    steps = 4
    part = rows // steps
    return pl.pallas_call(
        spread_kernel,
        grid_spec=pltpu.PrefetchScalarGridSpec(
            num_scalar_prefetch=1,
            grid=(steps,),
            in_specs=[
                pl.BlockSpec((part, classes), lambda i, p: (i, 0)),
                pl.BlockSpec((part, rank), lambda i, p: (i, 0)),
                pl.BlockSpec(mine.shape, lambda i, p: (0, 0, 0)),
                pl.BlockSpec(theirs.shape, lambda i, p: (0, 0, 0)),
            ],
            out_specs=[
                pl.BlockSpec((part, classes), lambda i, p: (i, 0)),
                pl.BlockSpec((part, classes), lambda i, p: (i, 0)),
                pl.BlockSpec((1, classes), lambda i, p: (0, 0)),
            ],
            scratch_shapes=[pltpu.VMEM((rank, classes), BF16)],
        ),
        out_shape=[
            jax.ShapeDtypeStruct((rows, classes), F32),
            jax.ShapeDtypeStruct((rows, classes), BF16),
            jax.ShapeDtypeStruct((1, classes), F32),
        ],
        compiler_params=pltpu.CompilerParams(vmem_limit_bytes=VMEM_LIMIT),
        name="spread",
    )(place, labels, basis, mine, theirs)


def apply_kernel(
    cols, valid, place, tiles, degree, search, own, l1, l2, l3, r1, r2, r3, image, dots, panel
):
    step = pl.program_id(0)
    slots, size, _ = tiles.shape
    rows = own.shape[0]
    me = place[2]
    last = panel.shape[0] // rows - 1

    @pl.when(step == 0)
    def _():
        dots[...] = jnp.zeros_like(dots)
        panel[pl.ds(pl.multiple_of(me * rows, rows), rows), :] = own[...]
        for k, (left, right) in enumerate(((l1, r1), (l2, r2), (l3, r3)), 1):

            @pl.when(me >= k)
            def _(left=left, k=k):
                panel[pl.ds(pl.multiple_of((me - k) * rows, rows), rows), :] = left[...]

            @pl.when(me + k <= last)
            def _(right=right, k=k):
                panel[pl.ds(pl.multiple_of((me + k) * rows, rows), rows), :] = right[...]

    total = jnp.zeros(search.shape, F32)
    for t in range(slots):
        at = step * slots + t
        block = panel[pl.ds(pl.multiple_of(cols[at] * size, size), size), :]
        product = jnp.dot(tiles[t], block, preferred_element_type=F32)
        total = total + product * valid[at].astype(F32)
    value = search[...]
    result = value + 0.5 * (degree[...] * value - total)
    image[...] = result
    dots[...] += jnp.sum(value * result, axis=0, keepdims=True)


def apply(cols, valid, place, tiles, degree, search, own, received, slots):
    rows, classes = search.shape
    count, size, _ = tiles.shape
    steps = count // slots
    whole = pl.BlockSpec((rows, classes), lambda i, c, v, p: (0, 0))
    return pl.pallas_call(
        apply_kernel,
        grid_spec=pltpu.PrefetchScalarGridSpec(
            num_scalar_prefetch=3,
            grid=(steps,),
            in_specs=[
                pl.BlockSpec((slots, size, size), lambda i, c, v, p: (i, 0, 0)),
                pl.BlockSpec((size, 1), lambda i, c, v, p: (i, 0)),
                pl.BlockSpec((size, classes), lambda i, c, v, p: (i, 0)),
            ]
            + [whole] * 7,
            out_specs=[
                pl.BlockSpec((size, classes), lambda i, c, v, p: (i, 0)),
                pl.BlockSpec((1, classes), lambda i, c, v, p: (0, 0)),
            ],
            scratch_shapes=[pltpu.VMEM((4 * rows, classes), BF16)],
        ),
        out_shape=[
            jax.ShapeDtypeStruct((rows, classes), F32),
            jax.ShapeDtypeStruct((1, classes), F32),
        ],
        compiler_params=pltpu.CompilerParams(vmem_limit_bytes=VMEM_LIMIT),
        name="apply",
    )(cols, valid, place, tiles, degree, search, own, *received)


def step_kernel(sums, labels, search, image, solution_out, residual_out):
    size = sums[0:1, :] / sums[1:2, :]
    solution_out[...] = size * search[...]
    residual_out[...] = labels[...].astype(F32) - size * image[...]


def take_step(sums, labels, search, image):
    rows, classes = search.shape
    steps = 4
    part = rows // steps
    block = pl.BlockSpec((part, classes), lambda i: (i, 0))
    return pl.pallas_call(
        step_kernel,
        grid=(steps,),
        in_specs=[pl.BlockSpec(sums.shape, lambda i: (0, 0)), block, block, block],
        out_specs=[block, block],
        out_shape=[jax.ShapeDtypeStruct((rows, classes), F32)] * 2,
        compiler_params=pltpu.CompilerParams(vmem_limit_bytes=VMEM_LIMIT),
        name="take_step",
    )(sums, labels, search, image)


def on_device(labels, basis, gains, tiles, tile_cols, tile_valid):
    labels, basis, tiles = labels[0], basis[0], tiles[0]
    rows_dev, classes = labels.shape
    rank = basis.shape[1]
    row_blocks, slots, tile_size = tiles.shape[:3]
    group = lax.axis_size("blk")
    tiles = tiles.reshape(row_blocks * slots, tile_size, tile_size)
    cols = tile_cols.reshape(-1)
    valid = tile_valid.reshape(-1)
    blk, y, x, core = (lax.axis_index(a) for a in ("blk", "y", "x", "core"))
    place = jnp.stack([core, x, blk]).astype(jnp.int32)

    row_total, col_parts = degree_parts(tiles, cols, valid, row_blocks * group, slots)
    col_parts = col_parts.reshape(group * rows_dev // classes, classes)
    extra = rows_dev // classes

    partial = lax.dot_general(
        basis, labels, (((0,), (0,)), ((), ())), preferred_element_type=F32
    )
    share = partial
    for axis in ("core", "x", "y"):
        share = reduce_scatter(share, axis)
    share_rows = share.shape[0]

    def with_cols(k):
        part = lax.dynamic_slice_in_dim(col_parts, ((blk + k) % group) * extra, extra)
        return jnp.concatenate([share, part], axis=0)

    joined = with_cols(0)
    for part in [shift(with_cols(k), "blk", k) for k in range(1, group)]:
        joined = joined + part
    share = joined[:share_rows]
    share = share + shift(share, "zh", 1)
    degree = 0.5 * (row_total + joined[share_rows:].reshape(rows_dev, 1))

    offset = (core * lax.axis_size("x") + x) * (share_rows * lax.axis_size("y")) + y * share_rows
    local_gain = lax.dynamic_slice_in_dim(gains, offset, share_rows)
    coeffs = (local_gain[:, None] * share).astype(BF16)
    size_y = lax.axis_size("y")
    over_y = jnp.zeros((size_y * share_rows, classes), BF16)
    for k, part in enumerate([coeffs] + [shift(coeffs, "y", k) for k in range(1, size_y)]):
        over_y = lax.dynamic_update_slice_in_dim(
            over_y, part, ((y + size_y - k) % size_y) * share_rows, 0
        )
    size_x = lax.axis_size("x")
    mine = jnp.stack([over_y] + [shift(over_y, "x", k) for k in range(1, size_x)])
    theirs = shift(mine, "core", 1)

    search, rounded, dot_rz = spread(place, labels, basis, mine, theirs)
    l1, r1 = along_line(rounded, 1, 0), along_line(rounded, -1, 0)
    l2, r2 = along_line(l1, 1, 1), along_line(r1, -1, 1)
    l3, r3 = along_line(l2, 1, 2), along_line(r2, -1, 2)
    image, dot_image = apply(
        cols, valid, place, tiles, degree, search, rounded, (l1, l2, l3, r1, r2, r3), slots
    )
    sums = jnp.concatenate([dot_rz, dot_image], axis=0)
    for axis in ("core", "x", "y", "blk", "zh"):
        sums = all_sum(sums, axis)
    solution_out, residual_out = take_step(sums, labels, search, image)
    return solution_out[None], residual_out[None]


def solution(mesh):
    blk, sample = mesh.devices.shape
    fine = Mesh(mesh.devices.reshape(blk, 4, 4, 2, sample // 32), FINE)
    return jax.shard_map(
        on_device,
        mesh=fine,
        in_specs=(
            P(SAMPLE, "blk", None),
            P(SAMPLE, "blk", None),
            P(),
            P(SAMPLE, "blk", None, None, None),
            P(SAMPLE, "blk", None),
            P(SAMPLE, "blk", None),
        ),
        out_specs=(P(SAMPLE, "blk", None), P(SAMPLE, "blk", None)),
        check_vma=False,
    )
```

```python
import jax
import jax.numpy as jnp
from jax import lax
from jax.experimental import pallas as pl
from jax.experimental.pallas import tpu as pltpu
from jax.sharding import Mesh, PartitionSpec as P

F32 = jnp.float32
BF16 = jnp.bfloat16
FINE = ("blk", "y", "x", "zh", "core")
SAMPLE = ("y", "x", "zh", "core")
PLANE = ("y", "x")
COLUMN = ("blk", "zh")
VMEM_LIMIT = 48 * 1024 * 1024
FIRST_BLOCKS = 2
EARLY_BLOCKS = 3


def params():
    return pltpu.CompilerParams(vmem_limit_bytes=VMEM_LIMIT)


def shift(value, axis, by):
    size = lax.axis_size(axis)
    return lax.ppermute(value, axis, [(i, (i + by) % size) for i in range(size)])


def along_line(value, by, skip):
    size = lax.axis_size("blk")
    if by > 0:
        pairs = [(i, i + 1) for i in range(skip, size - 1)]
    else:
        pairs = [(i, i - 1) for i in range(1, size - skip)]
    return lax.ppermute(value, "blk", pairs)


def both_ways(pair, skip):
    return along_line(pair[0], 1, skip), along_line(pair[1], -1, skip)


def all_sum(value, axis):
    total = value
    for part in [shift(value, axis, k) for k in range(1, lax.axis_size(axis))]:
        total = total + part
    return total


def to_all(value, axes):
    copies = jnp.broadcast_to(value[None], (lax.axis_size(axes),) + value.shape)
    return lax.all_to_all(copies, axes, 0, 0)


def project_kernel(place, basis, labels, out):
    @pl.when(pl.program_id(0) == 0)
    def _():
        out[...] = jnp.zeros_like(out)

    out[...] += lax.dot_general(
        basis[...], labels[...], (((0,), (0,)), ((), ())), preferred_element_type=F32
    )


def project(place, basis, labels, own):
    rows, classes = labels.shape
    half = basis.shape[1] // 2
    steps = 4
    part = rows // steps
    side = (lambda i, p: (i, p[0])) if own else (lambda i, p: (i, 1 - p[0]))
    return pl.pallas_call(
        project_kernel,
        grid_spec=pltpu.PrefetchScalarGridSpec(
            num_scalar_prefetch=1,
            grid=(steps,),
            in_specs=[
                pl.BlockSpec((part, half), side),
                pl.BlockSpec((part, classes), lambda i, p: (i, 0)),
            ],
            out_specs=pl.BlockSpec((half, classes), lambda i, p: (0, 0)),
        ),
        out_shape=jax.ShapeDtypeStruct((half, classes), F32),
        compiler_params=params(),
        cost_estimate=pl.CostEstimate(
            flops=2 * rows * half * classes, bytes_accessed=4 * rows * half, transcendentals=0
        ),
        name="project_own" if own else "project_other",
    )(place, basis, labels)


def degree_parts_kernel(cols, valid, tiles, rows_out, cols_out):
    step = pl.program_id(0)
    slots = tiles.shape[0]

    @pl.when(step == 0)
    def _():
        cols_out[...] = jnp.zeros_like(cols_out)

    total = jnp.zeros(tiles.shape[1:], F32)
    for t in range(slots):
        at = step * slots + t
        tile = tiles[t].astype(F32) * valid[at].astype(F32)
        total = total + tile
        cols_out[pl.ds(cols[at], 1), :] += jnp.sum(tile, axis=0, keepdims=True)
    rows_out[...] = jnp.sum(total, axis=1, keepdims=True)


def degree_parts(tiles, cols, valid, col_blocks, slots):
    count, size, _ = tiles.shape
    steps = count // slots
    return pl.pallas_call(
        degree_parts_kernel,
        grid_spec=pltpu.PrefetchScalarGridSpec(
            num_scalar_prefetch=2,
            grid=(steps,),
            in_specs=[pl.BlockSpec((slots, size, size), lambda i, c, v: (i, 0, 0))],
            out_specs=[
                pl.BlockSpec((size, 1), lambda i, c, v: (i, 0)),
                pl.BlockSpec((col_blocks, size), lambda i, c, v: (0, 0)),
            ],
        ),
        out_shape=[
            jax.ShapeDtypeStruct((steps * size, 1), F32),
            jax.ShapeDtypeStruct((col_blocks, size), F32),
        ],
        cost_estimate=pl.CostEstimate(
            flops=4 * tiles.size, bytes_accessed=2 * tiles.size, transcendentals=0
        ),
        name="degree_parts",
    )(cols, valid, tiles)


def spread_of(basis_own, basis_other, mine, theirs):
    return jnp.dot(basis_own[...], mine[...], preferred_element_type=F32) + jnp.dot(
        basis_other[...], theirs[...], preferred_element_type=F32
    )


def near_kernel(place, *refs):
    sides, (mine, theirs), outs = refs[:10], refs[10:12], refs[12:]
    step = pl.program_id(0)
    for k, out in enumerate(outs):
        labels, own_a, other_a, own_b, other_b = sides[5 * k : 5 * k + 5]
        first = FIRST_BLOCKS

        @pl.when(step < first)
        def _(out=out, labels=labels, own=own_a, other=other_a):
            out[...] = (labels[...].astype(F32) + spread_of(own, other, mine, theirs)).astype(BF16)

        @pl.when(step >= first)
        def _(out=out, labels=labels, own=own_b, other=other_b):
            out[...] = (labels[...].astype(F32) + spread_of(own, other, mine, theirs)).astype(BF16)


def spread_near(place, labels, first, second, mine, theirs, part):
    rows, classes = labels[0].shape
    half = mine.shape[0]
    split = first[0].shape[0] // part
    block = pl.BlockSpec((part, classes), lambda i, p: (i, 0))
    before = lambda i: jnp.minimum(i, split - 1)
    after = lambda i: jnp.maximum(i - split, 0)
    specs = [
        block,
        pl.BlockSpec((part, half), lambda i, p: (before(i), p[0])),
        pl.BlockSpec((part, half), lambda i, p: (before(i), 1 - p[0])),
        pl.BlockSpec((part, half), lambda i, p: (after(i), p[0])),
        pl.BlockSpec((part, half), lambda i, p: (after(i), 1 - p[0])),
    ]
    whole = pl.BlockSpec(mine.shape, lambda i, p: (0, 0))
    operands = []
    for k in range(2):
        operands += [labels[k], first[k], first[k], second[k], second[k]]
    return pl.pallas_call(
        near_kernel,
        grid_spec=pltpu.PrefetchScalarGridSpec(
            num_scalar_prefetch=1,
            grid=(rows // part,),
            in_specs=specs * 2 + [whole, whole],
            out_specs=[block, block],
        ),
        out_shape=[jax.ShapeDtypeStruct((rows, classes), BF16)] * 2,
        compiler_params=params(),
        cost_estimate=pl.CostEstimate(
            flops=8 * rows * half * classes, bytes_accessed=16 * rows * half, transcendentals=0
        ),
        name="spread_near",
    )(place, *operands, mine, theirs)


def spread_kernel(place, labels, own, other, mine, theirs, search, rounded, dots):
    @pl.when(pl.program_id(0) == 0)
    def _():
        dots[...] = jnp.zeros_like(dots)

    residual = labels[...].astype(F32)
    value = residual + spread_of(own, other, mine, theirs)
    search[...] = value
    rounded[...] = value.astype(BF16)
    dots[...] += jnp.sum(residual * value, axis=0, keepdims=True)


def spread(place, labels, basis, mine, theirs, part):
    rows, classes = labels.shape
    half = mine.shape[0]
    block = pl.BlockSpec((part, classes), lambda i, p: (i, 0))
    whole = pl.BlockSpec(mine.shape, lambda i, p: (0, 0))
    return pl.pallas_call(
        spread_kernel,
        grid_spec=pltpu.PrefetchScalarGridSpec(
            num_scalar_prefetch=1,
            grid=(rows // part,),
            in_specs=[
                block,
                pl.BlockSpec((part, half), lambda i, p: (i, p[0])),
                pl.BlockSpec((part, half), lambda i, p: (i, 1 - p[0])),
                whole,
                whole,
            ],
            out_specs=[block, block, pl.BlockSpec((1, classes), lambda i, p: (0, 0))],
        ),
        out_shape=[
            jax.ShapeDtypeStruct((rows, classes), F32),
            jax.ShapeDtypeStruct((rows, classes), BF16),
            jax.ShapeDtypeStruct((1, classes), F32),
        ],
        compiler_params=params(),
        cost_estimate=pl.CostEstimate(
            flops=4 * rows * half * classes, bytes_accessed=16 * rows * half, transcendentals=0
        ),
        name="spread",
    )(place, labels, basis, basis, mine, theirs)


def distance_of(col, me, group_blocks):
    return lax.div(col, jnp.int32(group_blocks)) - me


def apply_kernel(cols, valid, place, tiles, degree, search, own, *rest):
    near, (image, panel) = rest[:-2], rest[-2:]
    step = pl.program_id(0)
    slots, size, _ = tiles.shape
    rows = own.shape[0]
    me = place[1]
    last = panel.shape[0] // rows - 1

    def put(owner, piece, start):
        at = pl.multiple_of(owner * rows + start, size)
        panel[pl.ds(at, piece.shape[0]), :] = piece[...]

    @pl.when(step == 0)
    def _():
        put(me, own, 0)
        for k in (1, 2):
            left_a, right_a, left_b, right_b = near[4 * (k - 1) : 4 * k]

            @pl.when(me >= k)
            def _(a=left_a, b=left_b, k=k):
                put(me - k, a, 0)
                put(me - k, b, a.shape[0])

            @pl.when(me + k <= last)
            def _(a=right_a, b=right_b, k=k):
                put(me + k, a, 0)
                put(me + k, b, a.shape[0])

    value = search[...]
    image[...] = value + 0.5 * (degree[...] * value)
    for t in range(slots):
        at = step * slots + t
        away = distance_of(cols[at], me, rows // size)

        @pl.when(jnp.logical_and(valid[at] != 0, jnp.logical_and(away <= 2, away >= -2)))
        def _(t=t, at=at):
            block = panel[pl.ds(pl.multiple_of(cols[at] * size, size), size), :]
            product = jnp.dot(tiles[t], block, preferred_element_type=F32)
            image[...] -= 0.5 * product


def apply_first(cols, valid, place, tiles, degree, search, own, near, slots):
    rows, classes = search.shape
    count, size, _ = tiles.shape
    return pl.pallas_call(
        apply_kernel,
        grid_spec=pltpu.PrefetchScalarGridSpec(
            num_scalar_prefetch=3,
            grid=(count // slots,),
            in_specs=[
                pl.BlockSpec((slots, size, size), lambda i, c, v, p: (i, 0, 0)),
                pl.BlockSpec((size, 1), lambda i, c, v, p: (i, 0)),
                pl.BlockSpec((size, classes), lambda i, c, v, p: (i, 0)),
                pl.BlockSpec((rows, classes), lambda i, c, v, p: (0, 0)),
            ]
            + [pl.BlockSpec(a.shape, lambda i, c, v, p: (0, 0)) for a in near],
            out_specs=pl.BlockSpec((size, classes), lambda i, c, v, p: (i, 0)),
            scratch_shapes=[pltpu.VMEM((4 * rows, classes), BF16)],
        ),
        out_shape=jax.ShapeDtypeStruct((rows, classes), F32),
        compiler_params=params(),
        cost_estimate=pl.CostEstimate(
            flops=2 * count * size * size * classes,
            bytes_accessed=20 * rows * classes,
            transcendentals=0,
        ),
        name="apply_first",
    )(cols, valid, place, tiles, degree, search, own, *near)


def apply_far_kernel(
    cols, valid, place, tiles, search, image_in, left_a, right_a, left_b, right_b, image, dots
):
    step = pl.program_id(0)
    slots, size, _ = tiles.shape
    me = place[1]
    blocks_a = left_a.shape[0] // size
    blocks = blocks_a + left_b.shape[0] // size

    @pl.when(step == 0)
    def _():
        dots[...] = jnp.zeros_like(dots)

    image[...] = image_in[...]
    for t in range(slots):
        at = step * slots + t
        col = cols[at]
        away = distance_of(col, me, blocks)
        inner = lax.rem(col, jnp.int32(blocks))
        for sign, first, second in ((-3, left_a, left_b), (3, right_a, right_b)):
            here = jnp.logical_and(valid[at] != 0, away == sign)

            @pl.when(jnp.logical_and(here, inner < blocks_a))
            def _(t=t, source=first, inner=inner):
                at_row = jnp.minimum(inner, blocks_a - 1) * size
                block = source[pl.ds(pl.multiple_of(at_row, size), size), :]
                image[...] -= 0.5 * jnp.dot(tiles[t], block, preferred_element_type=F32)

            @pl.when(jnp.logical_and(here, inner >= blocks_a))
            def _(t=t, source=second, inner=inner):
                at_row = jnp.maximum(inner - blocks_a, 0) * size
                block = source[pl.ds(pl.multiple_of(at_row, size), size), :]
                image[...] -= 0.5 * jnp.dot(tiles[t], block, preferred_element_type=F32)

    dots[...] += jnp.sum(search[...] * image[...], axis=0, keepdims=True)


def apply_far(cols, valid, place, tiles, search, image, far, slots):
    rows, classes = search.shape
    count, size, _ = tiles.shape
    block = pl.BlockSpec((size, classes), lambda i, c, v, p: (i, 0))
    return pl.pallas_call(
        apply_far_kernel,
        grid_spec=pltpu.PrefetchScalarGridSpec(
            num_scalar_prefetch=3,
            grid=(count // slots,),
            in_specs=[
                pl.BlockSpec((slots, size, size), lambda i, c, v, p: (i, 0, 0)),
                block,
                block,
            ]
            + [pl.BlockSpec(a.shape, lambda i, c, v, p: (0, 0)) for a in far],
            out_specs=[block, pl.BlockSpec((1, classes), lambda i, c, v, p: (0, 0))],
        ),
        out_shape=[
            jax.ShapeDtypeStruct((rows, classes), F32),
            jax.ShapeDtypeStruct((1, classes), F32),
        ],
        compiler_params=params(),
        name="apply_far",
    )(cols, valid, place, tiles, search, image, *far)


def step_kernel(sums, labels, search, image, solution_out, residual_out):
    total = jnp.sum(sums[...], axis=0)
    size = total[0:1, :] / total[1:2, :]
    solution_out[...] = size * search[...]
    residual_out[...] = labels[...].astype(F32) - size * image[...]


def take_step(sums, labels, search, image):
    rows, classes = search.shape
    steps = 4
    block = pl.BlockSpec((rows // steps, classes), lambda i: (i, 0))
    return pl.pallas_call(
        step_kernel,
        grid=(steps,),
        in_specs=[pl.BlockSpec(sums.shape, lambda i: (0, 0, 0)), block, block, block],
        out_specs=[block, block],
        out_shape=[jax.ShapeDtypeStruct((rows, classes), F32)] * 2,
        compiler_params=params(),
        name="take_step",
    )(sums, labels, search, image)


def on_device(labels, basis, gains, tiles, tile_cols, tile_valid):
    labels, basis, tiles = labels[0], basis[0], tiles[0]
    rows_dev, classes = labels.shape
    row_blocks, slots, tile_size = tiles.shape[:3]
    group = lax.axis_size("blk")
    tiles = tiles.reshape(row_blocks * slots, tile_size, tile_size)
    blk, y, x, core = (lax.axis_index(a) for a in ("blk", "y", "x", "core"))
    place = jnp.stack([core, blk]).astype(jnp.int32)
    early = EARLY_BLOCKS * tile_size

    first = FIRST_BLOCKS * tile_size
    near_first = both_ways((basis[:first], basis[:first]), 0)

    sent = shift(project(place, basis, labels, False), "core", 1)
    chip_sum = project(place, basis, labels, True) + sent
    half = chip_sum.shape[0]
    peers = lax.axis_size(PLANE)
    pieces = lax.all_to_all(chip_sum.reshape(peers, half // peers, classes), PLANE, 0, 0)
    share = jnp.sum(pieces, axis=0)
    share, near_first, later = lax.optimization_barrier(
        (share, near_first, (basis[first:early], labels[:early]))
    )
    near_second = both_ways((later[0], later[0]), 0)
    near_labels = both_ways((later[1], later[1]), 0)
    share = all_sum(share, "blk")
    share = share + shift(share, "zh", 1)
    share_rows = share.shape[0]
    offset = core * half + (y * lax.axis_size("x") + x) * share_rows
    local_gain = lax.dynamic_slice_in_dim(gains, offset, share_rows)
    coeffs = (local_gain[:, None] * share).astype(BF16)
    mine = to_all(coeffs, PLANE).reshape(half, classes)
    theirs = shift(mine, "core", 1)

    near = spread_near(place, near_labels, near_first, near_second, mine, theirs, tile_size)
    two_a = both_ways(near, 1)
    search, rounded, dot_rz = spread(place, labels, basis, mine, theirs, tile_size)
    rest = rounded[early:]
    one_b = both_ways((rest, rest), 0)
    two_b = both_ways(one_b, 1)
    three_a = both_ways(two_a, 2)
    three_b = both_ways(two_b, 2)

    tied_tiles, tied_cols, tied_valid, _ = lax.optimization_barrier(
        (tiles, tile_cols, tile_valid, dot_rz)
    )
    cols = tied_cols.reshape(-1)
    valid = tied_valid.reshape(-1)
    row_total, col_parts = degree_parts(tied_tiles, cols, valid, row_blocks * group, slots)
    col_parts = col_parts.reshape(group * rows_dev // classes, classes)
    extra = rows_dev // classes
    parts = [
        lax.dynamic_slice_in_dim(col_parts, ((blk + k) % group) * extra, extra)
        for k in range(group)
    ]
    col_total = parts[0]
    for part in [shift(parts[k], "blk", k) for k in range(1, group)]:
        col_total = col_total + part
    degree = 0.5 * (row_total + col_total.reshape(rows_dev, 1))

    image = apply_first(
        cols, valid, place, tied_tiles, degree, search, rounded,
        (*near, *one_b, *two_a, *two_b), slots,
    )
    image, dot_image = apply_far(
        cols, valid, place, tied_tiles, search, image, (*three_a, *three_b), slots
    )
    sums = jnp.concatenate([dot_rz, dot_image], axis=0)
    sums = jnp.sum(to_all(sums, ("y", "x", "core")), axis=0)
    sums = to_all(sums, COLUMN)
    solution_out, residual_out = take_step(sums, labels, search, image)
    return solution_out[None], residual_out[None]


def solution(mesh):
    blk, sample = mesh.devices.shape
    fine = Mesh(mesh.devices.reshape(blk, 4, 4, 2, sample // 32), FINE)
    return jax.shard_map(
        on_device,
        mesh=fine,
        in_specs=(
            P(SAMPLE, "blk", None),
            P(SAMPLE, "blk", None),
            P(),
            P(SAMPLE, "blk", None, None, None),
            P(SAMPLE, "blk", None),
            P(SAMPLE, "blk", None),
        ),
        out_specs=(P(SAMPLE, "blk", None), P(SAMPLE, "blk", None)),
        check_vma=False,
    )
```

```python
import functools

import jax
import jax.numpy as jnp
from jax import lax
from jax.experimental import pallas as pl
from jax.experimental.pallas import tpu as pltpu
from jax.sharding import Mesh, PartitionSpec as P

F32 = jnp.float32
BF16 = jnp.bfloat16
FINE = ("blk", "y", "x", "zh", "core")
SAMPLE = ("y", "x", "zh", "core")
PLANE = ("y", "x")
COLUMN = ("blk", "zh")
VMEM_LIMIT = 48 * 1024 * 1024
VMEM_ALL = 60 * 1024 * 1024
CHUNKS = 2


def params(limit=VMEM_LIMIT):
    return pltpu.CompilerParams(vmem_limit_bytes=limit)


def shift(value, axis, by):
    size = lax.axis_size(axis)
    return lax.ppermute(value, axis, [(i, (i + by) % size) for i in range(size)])


def along_line(value, by, skip):
    size = lax.axis_size("blk")
    if by > 0:
        pairs = [(i, i + 1) for i in range(skip, size - 1)]
    else:
        pairs = [(i, i - 1) for i in range(1, size - skip)]
    return lax.ppermute(value, "blk", pairs)


def both_ways(pair, skip):
    return along_line(pair[0], 1, skip), along_line(pair[1], -1, skip)


def all_sum(value, axis):
    total = value
    for part in [shift(value, axis, k) for k in range(1, lax.axis_size(axis))]:
        total = total + part
    return total


def to_all(value, axes):
    copies = jnp.broadcast_to(value[None], (lax.axis_size(axes),) + value.shape)
    return lax.all_to_all(copies, axes, 0, 0)


def project_kernel(place, basis, labels, out):
    @pl.when(pl.program_id(0) == 0)
    def _():
        out[...] = jnp.zeros_like(out)

    out[...] += lax.dot_general(
        basis[...], labels[...], (((0,), (0,)), ((), ())), preferred_element_type=F32
    )


def project(place, basis, labels, own):
    rows, classes = labels.shape
    half = basis.shape[1] // 2
    steps = 4
    part = rows // steps
    side = (lambda i, p: (i, p[0])) if own else (lambda i, p: (i, 1 - p[0]))
    return pl.pallas_call(
        project_kernel,
        grid_spec=pltpu.PrefetchScalarGridSpec(
            num_scalar_prefetch=1,
            grid=(steps,),
            in_specs=[
                pl.BlockSpec((part, half), side),
                pl.BlockSpec((part, classes), lambda i, p: (i, 0)),
            ],
            out_specs=pl.BlockSpec((half, classes), lambda i, p: (0, 0)),
        ),
        out_shape=jax.ShapeDtypeStruct((half, classes), F32),
        compiler_params=params(),
        cost_estimate=pl.CostEstimate(
            flops=2 * rows * half * classes, bytes_accessed=4 * rows * half, transcendentals=0
        ),
        name="project_own" if own else "project_other",
    )(place, basis, labels)


def degree_parts_kernel(cols, valid, tiles, rows_out, cols_out):
    step = pl.program_id(0)
    slots = tiles.shape[0]

    @pl.when(step == 0)
    def _():
        cols_out[...] = jnp.zeros_like(cols_out)

    total = jnp.zeros(tiles.shape[1:], F32)
    for t in range(slots):
        at = step * slots + t
        tile = tiles[t].astype(F32) * valid[at].astype(F32)
        total = total + tile
        cols_out[pl.ds(cols[at], 1), :] += jnp.sum(tile, axis=0, keepdims=True)
    rows_out[...] = jnp.sum(total, axis=1, keepdims=True)


def degree_parts(tiles, cols, valid, col_blocks, slots):
    count, size, _ = tiles.shape
    steps = count // slots
    return pl.pallas_call(
        degree_parts_kernel,
        grid_spec=pltpu.PrefetchScalarGridSpec(
            num_scalar_prefetch=2,
            grid=(steps,),
            in_specs=[pl.BlockSpec((slots, size, size), lambda i, c, v: (i, 0, 0))],
            out_specs=[
                pl.BlockSpec((size, 1), lambda i, c, v: (i, 0)),
                pl.BlockSpec((col_blocks, size), lambda i, c, v: (0, 0)),
            ],
        ),
        out_shape=[
            jax.ShapeDtypeStruct((steps * size, 1), F32),
            jax.ShapeDtypeStruct((col_blocks, size), F32),
        ],
        cost_estimate=pl.CostEstimate(
            flops=4 * tiles.size, bytes_accessed=2 * tiles.size, transcendentals=0
        ),
        name="degree_parts",
    )(cols, valid, tiles)


def spread_of(basis_own, basis_other, mine, theirs):
    return jnp.dot(basis_own[...], mine[...], preferred_element_type=F32) + jnp.dot(
        basis_other[...], theirs[...], preferred_element_type=F32
    )


def spread_kernel(place, labels, own, other, mine, theirs, search, rounded, dots):
    @pl.when(pl.program_id(0) == 0)
    def _():
        dots[...] = jnp.zeros_like(dots)

    residual = labels[...].astype(F32)
    value = residual + spread_of(own, other, mine, theirs)
    search[...] = value
    rounded[...] = value.astype(BF16)
    dots[...] += jnp.sum(residual * value, axis=0, keepdims=True)


def spread(place, labels, basis, mine, theirs, part, chunk):
    rows, classes = labels.shape
    half = mine.shape[0]
    width = classes // CHUNKS
    block = pl.BlockSpec((part, width), lambda i, p: (i, 0))
    columns = pl.BlockSpec((half, width), lambda i, p: (0, chunk))
    return pl.pallas_call(
        spread_kernel,
        grid_spec=pltpu.PrefetchScalarGridSpec(
            num_scalar_prefetch=1,
            grid=(rows // part,),
            in_specs=[
                pl.BlockSpec((part, width), lambda i, p: (i, chunk)),
                pl.BlockSpec((part, half), lambda i, p: (i, p[0])),
                pl.BlockSpec((part, half), lambda i, p: (i, 1 - p[0])),
                columns,
                columns,
            ],
            out_specs=[block, block, pl.BlockSpec((1, width), lambda i, p: (0, 0))],
        ),
        out_shape=[
            jax.ShapeDtypeStruct((rows, width), F32),
            jax.ShapeDtypeStruct((rows, width), BF16),
            jax.ShapeDtypeStruct((1, width), F32),
        ],
        compiler_params=params(),
        cost_estimate=pl.CostEstimate(
            flops=4 * rows * half * width, bytes_accessed=16 * rows * width, transcendentals=0
        ),
        name=f"spread_{chunk}",
    )(place, labels, basis, basis, mine, theirs)


def apply_kernel(places, cols, valid, place, tiles, degree, search, own, *rest):
    pieces, (image, dots, panel, sems) = rest[:-4], rest[-4:]
    step = pl.program_id(0)
    slots, size, _ = tiles.shape
    rows = own.shape[0]
    me = place[1]
    last = panel.shape[0] // rows - 1

    def copies(act):
        for k, (offset, start) in enumerate(places):
            owner = me + offset

            @pl.when(jnp.logical_and(owner >= 0, owner <= last))
            def _(k=k, owner=owner, start=start):
                at = pl.multiple_of(owner * rows + start, size)
                target = panel.at[pl.ds(at, pieces[k].shape[0]), :]
                act(pltpu.make_async_copy(pieces[k], target, sems.at[k]))

    @pl.when(step == 0)
    def _():
        copies(lambda copy: copy.start())
        dots[...] = jnp.zeros_like(dots)
        panel[pl.ds(pl.multiple_of(me * rows, size), rows), :] = own[...]
        copies(lambda copy: copy.wait())

    value = search[...]
    total = value + 0.5 * (degree[...] * value)
    for t in range(slots):
        at = step * slots + t
        block = panel[pl.ds(pl.multiple_of(cols[at] * size, size), size), :]
        product = jnp.dot(tiles[t], block, preferred_element_type=F32)
        total = total - (0.5 * valid[at].astype(F32)) * product
    image[...] = total
    dots[...] += jnp.sum(value * total, axis=0, keepdims=True)


def apply(cols, valid, place, tiles, degree, search, own, placed, slots, chunk):
    rows, classes = search.shape
    count, size, _ = tiles.shape
    block = pl.BlockSpec((size, classes), lambda i, c, v, p: (i, 0))
    places = tuple(item[:2] for item in placed)
    pieces = [item[2] for item in placed]
    return pl.pallas_call(
        functools.partial(apply_kernel, places),
        grid_spec=pltpu.PrefetchScalarGridSpec(
            num_scalar_prefetch=3,
            grid=(count // slots,),
            in_specs=[
                pl.BlockSpec((slots, size, size), lambda i, c, v, p: (i, 0, 0)),
                pl.BlockSpec((size, 1), lambda i, c, v, p: (i, 0)),
                block,
                pl.BlockSpec((rows, classes), lambda i, c, v, p: (0, 0)),
            ]
            + [pl.BlockSpec(memory_space=pl.ANY)] * len(pieces),
            out_specs=[block, pl.BlockSpec((1, classes), lambda i, c, v, p: (0, 0))],
            scratch_shapes=[
                pltpu.VMEM((lax.axis_size("blk") * rows, classes), BF16),
                pltpu.SemaphoreType.DMA((len(pieces),)),
            ],
        ),
        out_shape=[
            jax.ShapeDtypeStruct((rows, classes), F32),
            jax.ShapeDtypeStruct((1, classes), F32),
        ],
        compiler_params=params(VMEM_ALL),
        cost_estimate=pl.CostEstimate(
            flops=2 * count * size * size * classes,
            bytes_accessed=20 * rows * classes,
            transcendentals=0,
        ),
        name=f"apply_{chunk}",
    )(cols, valid, place, tiles, degree, search, own, *pieces)


def step_kernel(sums, labels, *refs):
    searches, images = refs[:CHUNKS], refs[CHUNKS : 2 * CHUNKS]
    solution_out, residual_out = refs[2 * CHUNKS :]
    total = jnp.sum(sums[...], axis=0)
    size = total[0:1, :] / total[1:2, :]
    width = searches[0].shape[1]
    for k in range(CHUNKS):
        at = slice(k * width, (k + 1) * width)
        solution_out[:, at] = size[:, at] * searches[k][...]
        residual_out[:, at] = labels[:, at].astype(F32) - size[:, at] * images[k][...]


def take_step(sums, labels, searches, images, part):
    rows, classes = labels.shape
    block = pl.BlockSpec((part, classes), lambda i: (i, 0))
    piece = pl.BlockSpec((part, classes // CHUNKS), lambda i: (i, 0))
    return pl.pallas_call(
        step_kernel,
        grid=(rows // part,),
        in_specs=[pl.BlockSpec(sums.shape, lambda i: (0, 0, 0)), block] + [piece] * 2 * CHUNKS,
        out_specs=[block, block],
        out_shape=[jax.ShapeDtypeStruct((rows, classes), F32)] * 2,
        compiler_params=params(),
        name="take_step",
    )(sums, labels, *searches, *images)


def on_device(labels, basis, gains, tiles, tile_cols, tile_valid):
    labels, basis, tiles = labels[0], basis[0], tiles[0]
    rows_dev, classes = labels.shape
    row_blocks, slots, tile_size = tiles.shape[:3]
    group = lax.axis_size("blk")
    tiles = tiles.reshape(row_blocks * slots, tile_size, tile_size)
    blk, y, x, core = (lax.axis_index(a) for a in ("blk", "y", "x", "core"))
    place = jnp.stack([core, blk]).astype(jnp.int32)

    cols = tile_cols.reshape(-1)
    valid = tile_valid.reshape(-1)

    sent = shift(project(place, basis, labels, False), "core", 1)
    chip_sum = project(place, basis, labels, True) + sent
    chip_sum, later_tiles = lax.optimization_barrier((chip_sum, tiles))
    row_total, col_parts = degree_parts(later_tiles, cols, valid, row_blocks * group, slots)
    extra = rows_dev // classes
    col_parts = col_parts.reshape(group * extra, classes)
    half = chip_sum.shape[0]
    peers = lax.axis_size(PLANE)
    pieces = lax.all_to_all(chip_sum.reshape(peers, half // peers, classes), PLANE, 0, 0)
    share = jnp.sum(pieces, axis=0)
    share, col_parts = lax.optimization_barrier((share, col_parts))
    share_rows = share.shape[0]

    def with_cols(k):
        part = lax.dynamic_slice_in_dim(col_parts, ((blk + k) % group) * extra, extra)
        return jnp.concatenate([share, part], axis=0)

    joined = with_cols(0)
    for part in [shift(with_cols(k), "blk", k) for k in range(1, group)]:
        joined = joined + part
    share = joined[:share_rows]
    share = share + shift(share, "zh", 1)
    degree = 0.5 * (row_total + joined[share_rows:].reshape(rows_dev, 1))
    offset = core * half + (y * lax.axis_size("x") + x) * share_rows
    local_gain = lax.dynamic_slice_in_dim(gains, offset, share_rows)
    coeffs = (local_gain[:, None] * share).astype(BF16)
    mine = to_all(coeffs, PLANE).reshape(half, classes)
    theirs = shift(mine, "core", 1)

    searches, images, dots = [], [], []
    for chunk in range(CHUNKS):
        search, rounded, dot_rz = spread(place, labels, basis, mine, theirs, tile_size, chunk)
        placed, pair = [], (rounded, rounded)
        for k in range(1, group):
            pair = both_ways(pair, k - 1)
            placed += [(-k, 0, pair[0]), (k, 0, pair[1])]
        image, dot_image = apply(
            cols, valid, place, tiles, degree, search, rounded, placed, slots, chunk
        )
        searches.append(search)
        images.append(image)
        dots.append(jnp.concatenate([dot_rz, dot_image], axis=0))
    sums = jnp.concatenate(dots, axis=1)
    sums = jnp.sum(to_all(sums, ("y", "x", "core")), axis=0)
    sums = to_all(sums, COLUMN)
    solution_out, residual_out = take_step(sums, labels, searches, images, tile_size)
    return solution_out[None], residual_out[None]


def solution(mesh):
    blk, sample = mesh.devices.shape
    fine = Mesh(mesh.devices.reshape(blk, 4, 4, 2, sample // 32), FINE)
    return jax.shard_map(
        on_device,
        mesh=fine,
        in_specs=(
            P(SAMPLE, "blk", None),
            P(SAMPLE, "blk", None),
            P(),
            P(SAMPLE, "blk", None, None, None),
            P(SAMPLE, "blk", None),
            P(SAMPLE, "blk", None),
        ),
        out_specs=(P(SAMPLE, "blk", None), P(SAMPLE, "blk", None)),
        check_vma=False,
    )
```

```python
import functools

import jax
import jax.numpy as jnp
from jax import lax
from jax.experimental import pallas as pl
from jax.experimental.pallas import tpu as pltpu
from jax.sharding import Mesh, PartitionSpec as P

F32 = jnp.float32
BF16 = jnp.bfloat16
FINE = ("blk", "y", "x", "zh", "core")
SAMPLE = ("y", "x", "zh", "core")
PLANE = ("y", "x")
COLUMN = ("blk", "zh")
VMEM_SOME = 16 * 1024 * 1024
VMEM_ALL = 60 * 1024 * 1024
CHUNKS = 2


def params(limit=VMEM_SOME):
    return pltpu.CompilerParams(vmem_limit_bytes=limit)


def shift(value, axis, by):
    size = lax.axis_size(axis)
    return lax.ppermute(value, axis, [(i, (i + by) % size) for i in range(size)])


def along_line(value, by, skip):
    size = lax.axis_size("blk")
    if by > 0:
        pairs = [(i, i + 1) for i in range(skip, size - 1)]
    else:
        pairs = [(i, i - 1) for i in range(1, size - skip)]
    return lax.ppermute(value, "blk", pairs)


def both_ways(pair, skip):
    return along_line(pair[0], 1, skip), along_line(pair[1], -1, skip)


def all_sum(value, axis):
    total = value
    for part in [shift(value, axis, k) for k in range(1, lax.axis_size(axis))]:
        total = total + part
    return total


def to_all(value, axes):
    copies = jnp.broadcast_to(value[None], (lax.axis_size(axes),) + value.shape)
    return lax.all_to_all(copies, axes, 0, 0)


def project_kernel(place, basis, labels, out):
    @pl.when(pl.program_id(0) == 0)
    def _():
        out[...] = jnp.zeros_like(out)

    out[...] += lax.dot_general(
        basis[...], labels[...], (((0,), (0,)), ((), ())), preferred_element_type=F32
    )


def project(place, basis, labels, own):
    rows, classes = labels.shape
    half = basis.shape[1] // 2
    steps = 4
    part = rows // steps
    side = (lambda i, p: (i, p[0])) if own else (lambda i, p: (i, 1 - p[0]))
    return pl.pallas_call(
        project_kernel,
        grid_spec=pltpu.PrefetchScalarGridSpec(
            num_scalar_prefetch=1,
            grid=(steps,),
            in_specs=[
                pl.BlockSpec((part, half), side),
                pl.BlockSpec((part, classes), lambda i, p: (i, 0)),
            ],
            out_specs=pl.BlockSpec((half, classes), lambda i, p: (0, 0)),
        ),
        out_shape=jax.ShapeDtypeStruct((half, classes), F32),
        compiler_params=params(),
        cost_estimate=pl.CostEstimate(
            flops=2 * rows * half * classes, bytes_accessed=4 * rows * half, transcendentals=0
        ),
        name="project_own" if own else "project_other",
    )(place, basis, labels)


def degree_parts_kernel(cols, valid, tiles, rows_out, cols_out):
    step = pl.program_id(0)
    slots = tiles.shape[0]

    @pl.when(step == 0)
    def _():
        cols_out[...] = jnp.zeros_like(cols_out)

    total = jnp.zeros(tiles.shape[1:], F32)
    for t in range(slots):
        at = step * slots + t
        tile = tiles[t].astype(F32) * valid[at].astype(F32)
        total = total + tile
        cols_out[pl.ds(cols[at], 1), :] += jnp.sum(tile, axis=0, keepdims=True)
    rows_out[...] = jnp.sum(total, axis=1, keepdims=True)


def degree_parts(tiles, cols, valid, col_blocks, slots):
    count, size, _ = tiles.shape
    steps = count // slots
    return pl.pallas_call(
        degree_parts_kernel,
        grid_spec=pltpu.PrefetchScalarGridSpec(
            num_scalar_prefetch=2,
            grid=(steps,),
            in_specs=[pl.BlockSpec((slots, size, size), lambda i, c, v: (i, 0, 0))],
            out_specs=[
                pl.BlockSpec((size, 1), lambda i, c, v: (i, 0)),
                pl.BlockSpec((col_blocks, size), lambda i, c, v: (0, 0)),
            ],
        ),
        out_shape=[
            jax.ShapeDtypeStruct((steps * size, 1), F32),
            jax.ShapeDtypeStruct((col_blocks, size), F32),
        ],
        cost_estimate=pl.CostEstimate(
            flops=4 * tiles.size, bytes_accessed=2 * tiles.size, transcendentals=0
        ),
        name="degree_parts",
    )(cols, valid, tiles)


def spread_of(basis_own, basis_other, mine, theirs):
    return jnp.dot(basis_own[...], mine[...], preferred_element_type=F32) + jnp.dot(
        basis_other[...], theirs[...], preferred_element_type=F32
    )


def moves(sources, targets, sems, size, count):
    return [
        pltpu.make_async_copy(
            sources.at[pl.ds(k * size, size), :], targets.at[pl.ds(k * size, size), :], sems.at[k]
        )
        for k in range(count)
    ]


def start_at(copies, step):
    for k, copy in enumerate(copies):
        pl.when(step == k)(copy.start)


def wait_at(copies, step):
    for k, copy in enumerate(copies):
        pl.when(step == k)(copy.wait)


def spread_kernel(
    place, labels, own, other, mine, theirs, search, rounded, dots, v_search, sems
):
    step, steps = pl.program_id(0), pl.num_programs(0)
    size = labels.shape[0]

    @pl.when(step == 0)
    def _():
        dots[...] = jnp.zeros_like(dots)

    residual = labels[...].astype(F32)
    value = residual + spread_of(own, other, mine, theirs)
    rounded[...] = value.astype(BF16)
    v_search[pl.ds(pl.multiple_of(step * size, size), size), :] = value
    dots[...] += jnp.sum(residual * value, axis=0, keepdims=True)
    stores = moves(v_search, search, sems, size, v_search.shape[0] // size)
    start_at(stores, step)

    @pl.when(step == steps - 1)
    def _():
        for copy in stores:
            copy.wait()


def spread(place, labels, basis, mine, theirs, part, chunk):
    rows, classes = labels.shape
    half = mine.shape[0]
    width = classes // CHUNKS
    block = pl.BlockSpec((part, width), lambda i, p: (i, 0))
    columns = pl.BlockSpec((half, width), lambda i, p: (0, chunk))
    return pl.pallas_call(
        spread_kernel,
        grid_spec=pltpu.PrefetchScalarGridSpec(
            num_scalar_prefetch=1,
            grid=(rows // part,),
            in_specs=[
                pl.BlockSpec((part, width), lambda i, p: (i, chunk)),
                pl.BlockSpec((part, half), lambda i, p: (i, p[0])),
                pl.BlockSpec((part, half), lambda i, p: (i, 1 - p[0])),
                columns,
                columns,
            ],
            out_specs=[
                pl.BlockSpec(memory_space=pltpu.HBM),
                block,
                pl.BlockSpec((1, width), lambda i, p: (0, 0)),
            ],
            scratch_shapes=[
                pltpu.VMEM((rows, width), F32),
                pltpu.SemaphoreType.DMA((rows // part,)),
            ],
        ),
        out_shape=[
            jax.ShapeDtypeStruct((rows, width), F32),
            jax.ShapeDtypeStruct((rows, width), BF16),
            jax.ShapeDtypeStruct((1, width), F32),
        ],
        compiler_params=params(),
        cost_estimate=pl.CostEstimate(
            flops=4 * rows * half * width, bytes_accessed=16 * rows * width, transcendentals=0
        ),
        name=f"spread_{chunk}",
    )(place, labels, basis, basis, mine, theirs)


def apply_kernel(places, cols, valid, place, tiles, degree, search, own, *rest):
    pieces, (image, dots, panel, v_search, v_image, sems, in_sems, out_sems) = rest[:-8], rest[-8:]
    step, steps = pl.program_id(0), pl.num_programs(0)
    slots, size, _ = tiles.shape
    rows = own.shape[0]
    me = place[1]
    last = panel.shape[0] // rows - 1

    def copies(act):
        for k, (offset, start) in enumerate(places):
            owner = me + offset

            @pl.when(jnp.logical_and(owner >= 0, owner <= last))
            def _(k=k, owner=owner, start=start):
                at = pl.multiple_of(owner * rows + start, size)
                target = panel.at[pl.ds(at, pieces[k].shape[0]), :]
                act(pltpu.make_async_copy(pieces[k], target, sems.at[k]))

    blocks = v_search.shape[0] // size
    loads = moves(search, v_search, in_sems, size, blocks)
    stores = moves(v_image, image, out_sems, size, blocks)

    @pl.when(step == 0)
    def _():
        copies(lambda copy: copy.start())
        for copy in loads:
            copy.start()
        dots[...] = jnp.zeros_like(dots)
        panel[pl.ds(pl.multiple_of(me * rows, size), rows), :] = own[...]
        copies(lambda copy: copy.wait())

    wait_at(loads, step)
    here = pl.ds(pl.multiple_of(step * size, size), size)
    value = v_search[here, :]
    total = value + 0.5 * (degree[...] * value)
    for t in range(slots):
        at = step * slots + t
        block = panel[pl.ds(pl.multiple_of(cols[at] * size, size), size), :]
        product = jnp.dot(tiles[t], block, preferred_element_type=F32)
        total = total - (0.5 * valid[at].astype(F32)) * product
    v_image[here, :] = total
    dots[...] += jnp.sum(value * total, axis=0, keepdims=True)
    start_at(stores, step)

    @pl.when(step == steps - 1)
    def _():
        for copy in stores:
            copy.wait()


def apply(cols, valid, place, tiles, degree, search, own, placed, slots, chunk):
    rows, classes = search.shape
    count, size, _ = tiles.shape
    in_hbm = pl.BlockSpec(memory_space=pltpu.HBM)
    places = tuple(item[:2] for item in placed)
    pieces = [item[2] for item in placed]
    return pl.pallas_call(
        functools.partial(apply_kernel, places),
        grid_spec=pltpu.PrefetchScalarGridSpec(
            num_scalar_prefetch=3,
            grid=(count // slots,),
            in_specs=[
                pl.BlockSpec((slots, size, size), lambda i, c, v, p: (i, 0, 0)),
                pl.BlockSpec((size, 1), lambda i, c, v, p: (i, 0)),
                in_hbm,
                pl.BlockSpec((rows, classes), lambda i, c, v, p: (0, 0)),
            ]
            + [pl.BlockSpec(memory_space=pl.ANY)] * len(pieces),
            out_specs=[in_hbm, pl.BlockSpec((1, classes), lambda i, c, v, p: (0, 0))],
            scratch_shapes=[
                pltpu.VMEM((lax.axis_size("blk") * rows, classes), BF16),
                pltpu.VMEM((rows, classes), F32),
                pltpu.VMEM((rows, classes), F32),
                pltpu.SemaphoreType.DMA((len(pieces),)),
                pltpu.SemaphoreType.DMA((count // slots,)),
                pltpu.SemaphoreType.DMA((count // slots,)),
            ],
        ),
        out_shape=[
            jax.ShapeDtypeStruct((rows, classes), F32),
            jax.ShapeDtypeStruct((1, classes), F32),
        ],
        compiler_params=params(),
        cost_estimate=pl.CostEstimate(
            flops=2 * count * size * size * classes,
            bytes_accessed=20 * rows * classes,
            transcendentals=0,
        ),
        name=f"apply_{chunk}",
    )(cols, valid, place, tiles, degree, search, own, *pieces)


def step_kernel(sums, labels, *refs):
    searches, images = refs[:CHUNKS], refs[CHUNKS : 2 * CHUNKS]
    solution_out, residual_out = refs[2 * CHUNKS :]
    total = jnp.sum(sums[...], axis=0)
    size = total[0:1, :] / total[1:2, :]
    width = searches[0].shape[1]
    for k in range(CHUNKS):
        at = slice(k * width, (k + 1) * width)
        solution_out[:, at] = size[:, at] * searches[k][...]
        residual_out[:, at] = labels[:, at].astype(F32) - size[:, at] * images[k][...]


def take_step(sums, labels, searches, images, part):
    rows, classes = labels.shape
    block = pl.BlockSpec((part, classes), lambda i: (i, 0))
    piece = pl.BlockSpec((part, classes // CHUNKS), lambda i: (i, 0))
    return pl.pallas_call(
        step_kernel,
        grid=(rows // part,),
        in_specs=[pl.BlockSpec(sums.shape, lambda i: (0, 0, 0)), block] + [piece] * 2 * CHUNKS,
        out_specs=[block, block],
        out_shape=[jax.ShapeDtypeStruct((rows, classes), F32)] * 2,
        compiler_params=params(VMEM_ALL),
        name="take_step",
    )(sums, labels, *searches, *images)


def on_device(labels, basis, gains, tiles, tile_cols, tile_valid):
    labels, basis, tiles = labels[0], basis[0], tiles[0]
    rows_dev, classes = labels.shape
    row_blocks, slots, tile_size = tiles.shape[:3]
    group = lax.axis_size("blk")
    tiles = tiles.reshape(row_blocks * slots, tile_size, tile_size)
    blk, y, x, core = (lax.axis_index(a) for a in ("blk", "y", "x", "core"))
    place = jnp.stack([core, blk]).astype(jnp.int32)

    cols = tile_cols.reshape(-1)
    valid = tile_valid.reshape(-1)

    sent = shift(project(place, basis, labels, False), "core", 1)
    chip_sum = project(place, basis, labels, True) + sent
    chip_sum, later_tiles = lax.optimization_barrier((chip_sum, tiles))
    row_total, col_parts = degree_parts(later_tiles, cols, valid, row_blocks * group, slots)
    extra = rows_dev // classes
    col_parts = col_parts.reshape(group * extra, classes)
    half = chip_sum.shape[0]
    peers = lax.axis_size(PLANE)
    pieces = lax.all_to_all(chip_sum.reshape(peers, half // peers, classes), PLANE, 0, 0)
    share = jnp.sum(pieces, axis=0)
    share, col_parts = lax.optimization_barrier((share, col_parts))
    share_rows = share.shape[0]

    def with_cols(k):
        part = lax.dynamic_slice_in_dim(col_parts, ((blk + k) % group) * extra, extra)
        return jnp.concatenate([share, part], axis=0)

    joined = with_cols(0)
    for part in [shift(with_cols(k), "blk", k) for k in range(1, group)]:
        joined = joined + part
    share = joined[:share_rows]
    share = share + shift(share, "zh", 1)
    degree = 0.5 * (row_total + joined[share_rows:].reshape(rows_dev, 1))
    offset = core * half + (y * lax.axis_size("x") + x) * share_rows
    local_gain = lax.dynamic_slice_in_dim(gains, offset, share_rows)
    coeffs = (local_gain[:, None] * share).astype(BF16)
    mine = to_all(coeffs, PLANE).reshape(half, classes)
    theirs = shift(mine, "core", 1)

    searches, images, dots = [], [], []
    for chunk in range(CHUNKS):
        search, rounded, dot_rz = spread(place, labels, basis, mine, theirs, tile_size, chunk)
        placed, pair = [], (rounded, rounded)
        for k in range(1, group):
            pair = both_ways(pair, k - 1)
            placed += [(-k, 0, pair[0]), (k, 0, pair[1])]
        image, dot_image = apply(
            cols, valid, place, tiles, degree, search, rounded, placed, slots, chunk
        )
        searches.append(search)
        images.append(image)
        dots.append(jnp.concatenate([dot_rz, dot_image], axis=0))
    sums = jnp.concatenate(dots, axis=1)
    sums = jnp.sum(to_all(sums, ("y", "x", "core")), axis=0)
    sums = to_all(sums, COLUMN)
    solution_out, residual_out = take_step(sums, labels, searches, images, tile_size)
    return solution_out[None], residual_out[None]


def solution(mesh):
    blk, sample = mesh.devices.shape
    fine = Mesh(mesh.devices.reshape(blk, 4, 4, 2, sample // 32), FINE)
    return jax.shard_map(
        on_device,
        mesh=fine,
        in_specs=(
            P(SAMPLE, "blk", None),
            P(SAMPLE, "blk", None),
            P(),
            P(SAMPLE, "blk", None, None, None),
            P(SAMPLE, "blk", None),
            P(SAMPLE, "blk", None),
        ),
        out_specs=(P(SAMPLE, "blk", None), P(SAMPLE, "blk", None)),
        check_vma=False,
    )
```

```python
import functools

import jax
import jax.numpy as jnp
from jax import lax
from jax.experimental import pallas as pl
from jax.experimental.pallas import tpu as pltpu
from jax.sharding import Mesh, PartitionSpec as P

F32 = jnp.float32
BF16 = jnp.bfloat16
FINE = ("blk", "y", "x", "zh", "core")
SAMPLE = ("y", "x", "zh", "core")
PLANE = ("y", "x")
COLUMN = ("blk", "zh")
VMEM_SOME = 16 * 1024 * 1024
VMEM_ALL = 60 * 1024 * 1024
CHUNKS = 2


def params(limit=VMEM_SOME):
    return pltpu.CompilerParams(vmem_limit_bytes=limit)


def shift(value, axis, by):
    size = lax.axis_size(axis)
    return lax.ppermute(value, axis, [(i, (i + by) % size) for i in range(size)])


def along_line(value, by, skip):
    size = lax.axis_size("blk")
    if by > 0:
        pairs = [(i, i + 1) for i in range(skip, size - 1)]
    else:
        pairs = [(i, i - 1) for i in range(1, size - skip)]
    return lax.ppermute(value, "blk", pairs)


def both_ways(pair, skip):
    return along_line(pair[0], 1, skip), along_line(pair[1], -1, skip)


def all_sum(value, axis):
    total = value
    for part in [shift(value, axis, k) for k in range(1, lax.axis_size(axis))]:
        total = total + part
    return total


def to_all(value, axes):
    copies = jnp.broadcast_to(value[None], (lax.axis_size(axes),) + value.shape)
    return lax.all_to_all(copies, axes, 0, 0)


def project_kernel(place, basis, labels, out):
    @pl.when(pl.program_id(0) == 0)
    def _():
        out[...] = jnp.zeros_like(out)

    out[...] += lax.dot_general(
        basis[...], labels[...], (((0,), (0,)), ((), ())), preferred_element_type=F32
    )


def project(place, basis, labels, own):
    rows, classes = labels.shape
    half = basis.shape[1] // 2
    steps = 1
    part = rows // steps
    side = (lambda i, p: (i, p[0])) if own else (lambda i, p: (i, 1 - p[0]))
    return pl.pallas_call(
        project_kernel,
        grid_spec=pltpu.PrefetchScalarGridSpec(
            num_scalar_prefetch=1,
            grid=(steps,),
            in_specs=[
                pl.BlockSpec((part, half), side),
                pl.BlockSpec((part, classes), lambda i, p: (i, 0)),
            ],
            out_specs=pl.BlockSpec((half, classes), lambda i, p: (0, 0)),
        ),
        out_shape=jax.ShapeDtypeStruct((half, classes), F32),
        compiler_params=params(),
        cost_estimate=pl.CostEstimate(
            flops=2 * rows * half * classes, bytes_accessed=4 * rows * half, transcendentals=0
        ),
        name="project_own" if own else "project_other",
    )(place, basis, labels)


def degree_parts_kernel(cols, valid, tiles, rows_out, cols_out):
    step = pl.program_id(0)
    slots = tiles.shape[0]

    @pl.when(step == 0)
    def _():
        cols_out[...] = jnp.zeros_like(cols_out)

    total = jnp.zeros(tiles.shape[1:], F32)
    for t in range(slots):
        at = step * slots + t
        tile = tiles[t].astype(F32) * valid[at].astype(F32)
        total = total + tile
        cols_out[pl.ds(cols[at], 1), :] += jnp.sum(tile, axis=0, keepdims=True)
    rows_out[...] = jnp.sum(total, axis=1, keepdims=True)


def degree_parts(tiles, cols, valid, col_blocks, slots):
    count, size, _ = tiles.shape
    steps = count // slots
    return pl.pallas_call(
        degree_parts_kernel,
        grid_spec=pltpu.PrefetchScalarGridSpec(
            num_scalar_prefetch=2,
            grid=(steps,),
            in_specs=[pl.BlockSpec((slots, size, size), lambda i, c, v: (i, 0, 0))],
            out_specs=[
                pl.BlockSpec((size, 1), lambda i, c, v: (i, 0)),
                pl.BlockSpec((col_blocks, size), lambda i, c, v: (0, 0)),
            ],
        ),
        out_shape=[
            jax.ShapeDtypeStruct((steps * size, 1), F32),
            jax.ShapeDtypeStruct((col_blocks, size), F32),
        ],
        cost_estimate=pl.CostEstimate(
            flops=4 * tiles.size, bytes_accessed=2 * tiles.size, transcendentals=0
        ),
        name="degree_parts",
    )(cols, valid, tiles)


def spread_of(basis_own, basis_other, mine, theirs):
    return jnp.dot(basis_own[...], mine[...], preferred_element_type=F32) + jnp.dot(
        basis_other[...], theirs[...], preferred_element_type=F32
    )


def moves(sources, targets, sems, size, count):
    return [
        pltpu.make_async_copy(
            sources.at[pl.ds(k * size, size), :], targets.at[pl.ds(k * size, size), :], sems.at[k]
        )
        for k in range(count)
    ]


def start_at(copies, step):
    for k, copy in enumerate(copies):
        pl.when(step == k)(copy.start)


def spread_kernel(
    place, labels, own, other, mine, theirs, search, rounded, dots, v_search, sems
):
    step, steps = pl.program_id(0), pl.num_programs(0)
    size = labels.shape[0]

    @pl.when(step == 0)
    def _():
        dots[...] = jnp.zeros_like(dots)

    residual = labels[...].astype(F32)
    value = residual + spread_of(own, other, mine, theirs)
    rounded[...] = value.astype(BF16)
    v_search[pl.ds(pl.multiple_of(step * size, size), size), :] = value
    dots[...] += jnp.sum(residual * value, axis=0, keepdims=True)
    stores = moves(v_search, search, sems, size, v_search.shape[0] // size)
    start_at(stores, step)

    @pl.when(step == steps - 1)
    def _():
        for copy in stores:
            copy.wait()


def spread(place, labels, basis, mine, theirs, part, chunk):
    rows, classes = labels.shape
    half = mine.shape[0]
    width = classes // CHUNKS
    block = pl.BlockSpec((part, width), lambda i, p: (i, 0))
    columns = pl.BlockSpec((half, width), lambda i, p: (0, chunk))
    return pl.pallas_call(
        spread_kernel,
        grid_spec=pltpu.PrefetchScalarGridSpec(
            num_scalar_prefetch=1,
            grid=(rows // part,),
            in_specs=[
                pl.BlockSpec((part, width), lambda i, p: (i, chunk)),
                pl.BlockSpec((part, half), lambda i, p: (i, p[0])),
                pl.BlockSpec((part, half), lambda i, p: (i, 1 - p[0])),
                columns,
                columns,
            ],
            out_specs=[
                pl.BlockSpec(memory_space=pltpu.HBM),
                block,
                pl.BlockSpec((1, width), lambda i, p: (0, 0)),
            ],
            scratch_shapes=[
                pltpu.VMEM((rows, width), F32),
                pltpu.SemaphoreType.DMA((rows // part,)),
            ],
        ),
        out_shape=[
            jax.ShapeDtypeStruct((rows, width), F32),
            jax.ShapeDtypeStruct((rows, width), BF16),
            jax.ShapeDtypeStruct((1, width), F32),
        ],
        compiler_params=params(),
        cost_estimate=pl.CostEstimate(
            flops=4 * rows * half * width, bytes_accessed=16 * rows * width, transcendentals=0
        ),
        name=f"spread_{chunk}",
    )(place, labels, basis, basis, mine, theirs)


def apply_kernel(places, cols, valid, place, tiles, degree, search, own, *rest):
    pieces, (image, dots, panel, v_search, v_image, sems, in_sems, out_sems) = rest[:-8], rest[-8:]
    count, size, _ = tiles.shape
    rows = own.shape[0]
    blocks = rows // size
    slots = count // blocks
    me = place[1]
    last = panel.shape[0] // rows - 1

    def copies(act):
        for k, (offset, start) in enumerate(places):
            owner = me + offset

            @pl.when(jnp.logical_and(owner >= 0, owner <= last))
            def _(k=k, owner=owner, start=start):
                at = pl.multiple_of(owner * rows + start, size)
                target = panel.at[pl.ds(at, pieces[k].shape[0]), :]
                act(pltpu.make_async_copy(pieces[k], target, sems.at[k]))

    copies(lambda copy: copy.start())
    loads = moves(search, v_search, in_sems, size, blocks)
    stores = moves(v_image, image, out_sems, size, blocks)
    for copy in loads:
        copy.start()
    panel[pl.ds(pl.multiple_of(me * rows, size), rows), :] = own[...]
    copies(lambda copy: copy.wait())
    sums = jnp.zeros(dots.shape, F32)
    for b in range(blocks):
        loads[b].wait()
        here = pl.ds(b * size, size)
        value = v_search[here, :]
        total = value + 0.5 * (degree[here, :] * value)
        for t in range(b * slots, (b + 1) * slots):
            block = panel[pl.ds(pl.multiple_of(cols[t] * size, size), size), :]
            product = jnp.dot(tiles[t], block, preferred_element_type=F32)
            total = total - (0.5 * valid[t].astype(F32)) * product
        v_image[here, :] = total
        stores[b].start()
        sums = sums + jnp.sum(value * total, axis=0, keepdims=True)
    dots[...] = sums
    for copy in stores:
        copy.wait()


def apply(cols, valid, place, tiles, degree, search, own, placed, slots, chunk):
    rows, classes = search.shape
    count, size, _ = tiles.shape
    in_hbm = pl.BlockSpec(memory_space=pltpu.HBM)
    places = tuple(item[:2] for item in placed)
    pieces = [item[2] for item in placed]
    return pl.pallas_call(
        functools.partial(apply_kernel, places),
        grid_spec=pltpu.PrefetchScalarGridSpec(
            num_scalar_prefetch=3,
            grid=(1,),
            in_specs=[
                pl.BlockSpec(tiles.shape, lambda i, c, v, p: (0, 0, 0)),
                pl.BlockSpec((rows, 1), lambda i, c, v, p: (0, 0)),
                in_hbm,
                pl.BlockSpec((rows, classes), lambda i, c, v, p: (0, 0)),
            ]
            + [pl.BlockSpec(memory_space=pl.ANY)] * len(pieces),
            out_specs=[in_hbm, pl.BlockSpec((1, classes), lambda i, c, v, p: (0, 0))],
            scratch_shapes=[
                pltpu.VMEM((lax.axis_size("blk") * rows, classes), BF16),
                pltpu.VMEM((rows, classes), F32),
                pltpu.VMEM((rows, classes), F32),
                pltpu.SemaphoreType.DMA((len(pieces),)),
                pltpu.SemaphoreType.DMA((count // slots,)),
                pltpu.SemaphoreType.DMA((count // slots,)),
            ],
        ),
        out_shape=[
            jax.ShapeDtypeStruct((rows, classes), F32),
            jax.ShapeDtypeStruct((1, classes), F32),
        ],
        compiler_params=params(),
        cost_estimate=pl.CostEstimate(
            flops=2 * count * size * size * classes,
            bytes_accessed=20 * rows * classes,
            transcendentals=0,
        ),
        name=f"apply_{chunk}",
    )(cols, valid, place, tiles, degree, search, own, *pieces)


def step_kernel(sums, labels, *refs):
    searches, images = refs[:CHUNKS], refs[CHUNKS : 2 * CHUNKS]
    solution_out, residual_out = refs[2 * CHUNKS :]
    total = jnp.sum(sums[...], axis=0)
    size = total[0:1, :] / total[1:2, :]
    width = searches[0].shape[1]
    for k in range(CHUNKS):
        at = slice(k * width, (k + 1) * width)
        solution_out[:, at] = size[:, at] * searches[k][...]
        residual_out[:, at] = labels[:, at].astype(F32) - size[:, at] * images[k][...]


def take_step(sums, labels, searches, images, part):
    rows, classes = labels.shape
    block = pl.BlockSpec((part, classes), lambda i: (i, 0))
    piece = pl.BlockSpec((part, classes // CHUNKS), lambda i: (i, 0))
    return pl.pallas_call(
        step_kernel,
        grid=(rows // part,),
        in_specs=[pl.BlockSpec(sums.shape, lambda i: (0, 0, 0)), block] + [piece] * 2 * CHUNKS,
        out_specs=[block, block],
        out_shape=[jax.ShapeDtypeStruct((rows, classes), F32)] * 2,
        compiler_params=params(VMEM_ALL),
        name="take_step",
    )(sums, labels, *searches, *images)


def on_device(labels, basis, gains, tiles, tile_cols, tile_valid):
    labels, basis, tiles = labels[0], basis[0], tiles[0]
    rows_dev, classes = labels.shape
    row_blocks, slots, tile_size = tiles.shape[:3]
    group = lax.axis_size("blk")
    tiles = tiles.reshape(row_blocks * slots, tile_size, tile_size)
    blk, y, x, core = (lax.axis_index(a) for a in ("blk", "y", "x", "core"))
    place = jnp.stack([core, blk]).astype(jnp.int32)

    cols = tile_cols.reshape(-1)
    valid = tile_valid.reshape(-1)

    sent = shift(project(place, basis, labels, False), "core", 1)
    chip_sum = project(place, basis, labels, True) + sent
    chip_sum, later_tiles = lax.optimization_barrier((chip_sum, tiles))
    row_total, col_parts = degree_parts(later_tiles, cols, valid, row_blocks * group, slots)
    extra = rows_dev // classes
    col_parts = col_parts.reshape(group * extra, classes)
    half = chip_sum.shape[0]
    peers = lax.axis_size(PLANE)
    pieces = lax.all_to_all(chip_sum.reshape(peers, half // peers, classes), PLANE, 0, 0)
    share = jnp.sum(pieces, axis=0)
    share, col_parts = lax.optimization_barrier((share, col_parts))
    share_rows = share.shape[0]

    def with_cols(k):
        part = lax.dynamic_slice_in_dim(col_parts, ((blk + k) % group) * extra, extra)
        return jnp.concatenate([share, part], axis=0)

    joined = with_cols(0)
    for part in [shift(with_cols(k), "blk", k) for k in range(1, group)]:
        joined = joined + part
    share = joined[:share_rows]
    share = share + shift(share, "zh", 1)
    degree = 0.5 * (row_total + joined[share_rows:].reshape(rows_dev, 1))
    offset = core * half + (y * lax.axis_size("x") + x) * share_rows
    local_gain = lax.dynamic_slice_in_dim(gains, offset, share_rows)
    coeffs = (local_gain[:, None] * share).astype(BF16)
    mine = to_all(coeffs, PLANE).reshape(half, classes)
    theirs = shift(mine, "core", 1)

    searches, images, dots = [], [], []
    for chunk in range(CHUNKS):
        search, rounded, dot_rz = spread(place, labels, basis, mine, theirs, rows_dev // 2, chunk)
        placed, pair = [], (rounded, rounded)
        for k in range(1, group):
            pair = both_ways(pair, k - 1)
            placed += [(-k, 0, pair[0]), (k, 0, pair[1])]
        image, dot_image = apply(
            cols, valid, place, tiles, degree, search, rounded, placed, slots, chunk
        )
        searches.append(search)
        images.append(image)
        dots.append(jnp.concatenate([dot_rz, dot_image], axis=0))
    sums = jnp.concatenate(dots, axis=1)
    sums = jnp.sum(to_all(sums, ("y", "x", "core")), axis=0)
    sums = to_all(sums, COLUMN)
    solution_out, residual_out = take_step(sums, labels, searches, images, rows_dev // 2)
    return solution_out[None], residual_out[None]


def solution(mesh):
    blk, sample = mesh.devices.shape
    fine = Mesh(mesh.devices.reshape(blk, 4, 4, 2, sample // 32), FINE)
    return jax.shard_map(
        on_device,
        mesh=fine,
        in_specs=(
            P(SAMPLE, "blk", None),
            P(SAMPLE, "blk", None),
            P(),
            P(SAMPLE, "blk", None, None, None),
            P(SAMPLE, "blk", None),
            P(SAMPLE, "blk", None),
        ),
        out_specs=(P(SAMPLE, "blk", None), P(SAMPLE, "blk", None)),
        check_vma=False,
    )
```

```python
import functools

import jax
import jax.numpy as jnp
from jax import lax
from jax.experimental import pallas as pl
from jax.experimental.pallas import tpu as pltpu
from jax.sharding import Mesh, PartitionSpec as P

F32 = jnp.float32
BF16 = jnp.bfloat16
FINE = ("blk", "y", "x", "zh", "core")
SAMPLE = ("y", "x", "zh", "core")
PLANE = ("y", "x")
COLUMN = ("blk", "zh")
VMEM_SOME = 32 * 1024 * 1024
VMEM_ALL = 60 * 1024 * 1024
CHUNKS = 2


def params(limit=VMEM_SOME):
    return pltpu.CompilerParams(vmem_limit_bytes=limit)


def shift(value, axis, by):
    size = lax.axis_size(axis)
    return lax.ppermute(value, axis, [(i, (i + by) % size) for i in range(size)])


def along_line(value, by, skip):
    size = lax.axis_size("blk")
    if by > 0:
        pairs = [(i, i + 1) for i in range(skip, size - 1)]
    else:
        pairs = [(i, i - 1) for i in range(1, size - skip)]
    return lax.ppermute(value, "blk", pairs)


def both_ways(pair, skip):
    return along_line(pair[0], 1, skip), along_line(pair[1], -1, skip)


def all_sum(value, axis):
    total = value
    for part in [shift(value, axis, k) for k in range(1, lax.axis_size(axis))]:
        total = total + part
    return total


def to_all(value, axes):
    copies = jnp.broadcast_to(value[None], (lax.axis_size(axes),) + value.shape)
    return lax.all_to_all(copies, axes, 0, 0)


def project_kernel(place, basis, labels, out):
    @pl.when(pl.program_id(0) == 0)
    def _():
        out[...] = jnp.zeros_like(out)

    out[...] += lax.dot_general(
        basis[...], labels[...], (((0,), (0,)), ((), ())), preferred_element_type=F32
    )


def project(place, basis, labels, own):
    rows, classes = labels.shape
    half = basis.shape[1] // 2
    steps = 1
    part = rows // steps
    side = (lambda i, p: (i, p[0])) if own else (lambda i, p: (i, 1 - p[0]))
    return pl.pallas_call(
        project_kernel,
        grid_spec=pltpu.PrefetchScalarGridSpec(
            num_scalar_prefetch=1,
            grid=(steps,),
            in_specs=[
                pl.BlockSpec((part, half), side),
                pl.BlockSpec((part, classes), lambda i, p: (i, 0)),
            ],
            out_specs=pl.BlockSpec((half, classes), lambda i, p: (0, 0)),
        ),
        out_shape=jax.ShapeDtypeStruct((half, classes), F32),
        compiler_params=params(),
        cost_estimate=pl.CostEstimate(
            flops=2 * rows * half * classes, bytes_accessed=4 * rows * half, transcendentals=0
        ),
        name="project_own" if own else "project_other",
    )(place, basis, labels)


def degree_parts_kernel(cols, valid, tiles, rows_out, cols_out):
    step = pl.program_id(0)
    slots = tiles.shape[0]

    @pl.when(step == 0)
    def _():
        cols_out[...] = jnp.zeros_like(cols_out)

    total = jnp.zeros(tiles.shape[1:], F32)
    for t in range(slots):
        at = step * slots + t
        tile = tiles[t].astype(F32) * valid[at].astype(F32)
        total = total + tile
        cols_out[pl.ds(cols[at], 1), :] += jnp.sum(tile, axis=0, keepdims=True)
    rows_out[...] = jnp.sum(total, axis=1, keepdims=True)


def degree_parts(tiles, cols, valid, col_blocks, slots):
    count, size, _ = tiles.shape
    steps = count // slots
    return pl.pallas_call(
        degree_parts_kernel,
        grid_spec=pltpu.PrefetchScalarGridSpec(
            num_scalar_prefetch=2,
            grid=(steps,),
            in_specs=[pl.BlockSpec((slots, size, size), lambda i, c, v: (i, 0, 0))],
            out_specs=[
                pl.BlockSpec((size, 1), lambda i, c, v: (i, 0)),
                pl.BlockSpec((col_blocks, size), lambda i, c, v: (0, 0)),
            ],
        ),
        out_shape=[
            jax.ShapeDtypeStruct((steps * size, 1), F32),
            jax.ShapeDtypeStruct((col_blocks, size), F32),
        ],
        cost_estimate=pl.CostEstimate(
            flops=4 * tiles.size, bytes_accessed=2 * tiles.size, transcendentals=0
        ),
        name="degree_parts",
    )(cols, valid, tiles)


def spread_of(basis_own, basis_other, mine, theirs):
    return jnp.dot(basis_own[...], mine[...], preferred_element_type=F32) + jnp.dot(
        basis_other[...], theirs[...], preferred_element_type=F32
    )


def moves(sources, targets, sems, size, count):
    return [
        pltpu.make_async_copy(
            sources.at[pl.ds(k * size, size), :], targets.at[pl.ds(k * size, size), :], sems.at[k]
        )
        for k in range(count)
    ]


def start_at(copies, step):
    for k, copy in enumerate(copies):
        pl.when(step == k)(copy.start)


def spread_kernel(
    place, labels, own, other, mine, theirs, search, rounded, dots, v_search, sems
):
    step, steps = pl.program_id(0), pl.num_programs(0)
    size = labels.shape[0]

    @pl.when(step == 0)
    def _():
        dots[...] = jnp.zeros_like(dots)

    residual = labels[...].astype(F32)
    value = residual + spread_of(own, other, mine, theirs)
    rounded[...] = value.astype(BF16)
    v_search[pl.ds(pl.multiple_of(step * size, size), size), :] = value
    dots[...] += jnp.sum(residual * value, axis=0, keepdims=True)
    stores = moves(v_search, search, sems, size, v_search.shape[0] // size)
    start_at(stores, step)

    @pl.when(step == steps - 1)
    def _():
        for copy in stores:
            copy.wait()


def spread(place, labels, basis, mine, theirs, part, chunk):
    rows, classes = labels.shape
    half = mine.shape[0]
    width = classes // CHUNKS
    block = pl.BlockSpec((part, width), lambda i, p: (i, 0))
    columns = pl.BlockSpec((half, width), lambda i, p: (0, chunk))
    return pl.pallas_call(
        spread_kernel,
        grid_spec=pltpu.PrefetchScalarGridSpec(
            num_scalar_prefetch=1,
            grid=(rows // part,),
            in_specs=[
                pl.BlockSpec((part, width), lambda i, p: (i, chunk)),
                pl.BlockSpec((part, half), lambda i, p: (i, p[0])),
                pl.BlockSpec((part, half), lambda i, p: (i, 1 - p[0])),
                columns,
                columns,
            ],
            out_specs=[
                pl.BlockSpec(memory_space=pltpu.HBM),
                block,
                pl.BlockSpec((1, width), lambda i, p: (0, 0)),
            ],
            scratch_shapes=[
                pltpu.VMEM((rows, width), F32),
                pltpu.SemaphoreType.DMA((rows // part,)),
            ],
        ),
        out_shape=[
            jax.ShapeDtypeStruct((rows, width), F32),
            jax.ShapeDtypeStruct((rows, width), BF16),
            jax.ShapeDtypeStruct((1, width), F32),
        ],
        compiler_params=params(),
        cost_estimate=pl.CostEstimate(
            flops=4 * rows * half * width, bytes_accessed=16 * rows * width, transcendentals=0
        ),
        name=f"spread_{chunk}",
    )(place, labels, basis, basis, mine, theirs)


def apply_kernel(places, cols, valid, place, tiles, degree, search, own, *rest):
    pieces, (image, dots, panel, v_search, v_image, sems, in_sems, out_sems) = rest[:-8], rest[-8:]
    count, size, _ = tiles.shape
    rows = own.shape[0]
    blocks = rows // size
    slots = count // blocks
    me = place[1]
    last = panel.shape[0] // rows - 1

    def copies(act):
        for k, (offset, start) in enumerate(places):
            owner = me + offset

            @pl.when(jnp.logical_and(owner >= 0, owner <= last))
            def _(k=k, owner=owner, start=start):
                at = pl.multiple_of(owner * rows + start, size)
                target = panel.at[pl.ds(at, pieces[k].shape[0]), :]
                act(pltpu.make_async_copy(pieces[k], target, sems.at[k]))

    copies(lambda copy: copy.start())
    loads = moves(search, v_search, in_sems, size, blocks)
    stores = moves(v_image, image, out_sems, size, blocks)
    for copy in loads:
        copy.start()
    panel[pl.ds(pl.multiple_of(me * rows, size), rows), :] = own[...]
    copies(lambda copy: copy.wait())
    sums = jnp.zeros(dots.shape, F32)
    for b in range(blocks):
        loads[b].wait()
        here = pl.ds(b * size, size)
        value = v_search[here, :]
        total = value + 0.5 * (degree[here, :] * value)
        for t in range(b * slots, (b + 1) * slots):
            block = panel[pl.ds(pl.multiple_of(cols[t] * size, size), size), :]
            product = jnp.dot(tiles[t], block, preferred_element_type=F32)
            total = total - (0.5 * valid[t].astype(F32)) * product
        v_image[here, :] = total
        stores[b].start()
        sums = sums + jnp.sum(value * total, axis=0, keepdims=True)
    dots[...] = sums
    for copy in stores:
        copy.wait()


def apply(cols, valid, place, tiles, degree, search, own, placed, slots, chunk):
    rows, classes = search.shape
    count, size, _ = tiles.shape
    in_hbm = pl.BlockSpec(memory_space=pltpu.HBM)
    places = tuple(item[:2] for item in placed)
    pieces = [item[2] for item in placed]
    return pl.pallas_call(
        functools.partial(apply_kernel, places),
        grid_spec=pltpu.PrefetchScalarGridSpec(
            num_scalar_prefetch=3,
            grid=(1,),
            in_specs=[
                pl.BlockSpec(tiles.shape, lambda i, c, v, p: (0, 0, 0)),
                pl.BlockSpec((rows, 1), lambda i, c, v, p: (0, 0)),
                in_hbm,
                pl.BlockSpec((rows, classes), lambda i, c, v, p: (0, 0)),
            ]
            + [pl.BlockSpec(memory_space=pl.ANY)] * len(pieces),
            out_specs=[in_hbm, pl.BlockSpec((1, classes), lambda i, c, v, p: (0, 0))],
            scratch_shapes=[
                pltpu.VMEM((lax.axis_size("blk") * rows, classes), BF16),
                pltpu.VMEM((rows, classes), F32),
                pltpu.VMEM((rows, classes), F32),
                pltpu.SemaphoreType.DMA((len(pieces),)),
                pltpu.SemaphoreType.DMA((count // slots,)),
                pltpu.SemaphoreType.DMA((count // slots,)),
            ],
        ),
        out_shape=[
            jax.ShapeDtypeStruct((rows, classes), F32),
            jax.ShapeDtypeStruct((1, classes), F32),
        ],
        compiler_params=params(),
        cost_estimate=pl.CostEstimate(
            flops=2 * count * size * size * classes,
            bytes_accessed=20 * rows * classes,
            transcendentals=0,
        ),
        name=f"apply_{chunk}",
    )(cols, valid, place, tiles, degree, search, own, *pieces)


def step_kernel(sums, labels, *refs):
    searches, images = refs[:CHUNKS], refs[CHUNKS : 2 * CHUNKS]
    solution_out, residual_out = refs[2 * CHUNKS :]
    total = jnp.sum(sums[...], axis=0)
    size = total[0:1, :] / total[1:2, :]
    width = searches[0].shape[1]
    for k in range(CHUNKS):
        at = slice(k * width, (k + 1) * width)
        solution_out[:, at] = size[:, at] * searches[k][...]
        residual_out[:, at] = labels[:, at].astype(F32) - size[:, at] * images[k][...]


def take_step(sums, labels, searches, images, part):
    rows, classes = labels.shape
    block = pl.BlockSpec((part, classes), lambda i: (i, 0))
    piece = pl.BlockSpec((part, classes // CHUNKS), lambda i: (i, 0))
    return pl.pallas_call(
        step_kernel,
        grid=(rows // part,),
        in_specs=[pl.BlockSpec(sums.shape, lambda i: (0, 0, 0)), block] + [piece] * 2 * CHUNKS,
        out_specs=[block, block],
        out_shape=[jax.ShapeDtypeStruct((rows, classes), F32)] * 2,
        compiler_params=params(VMEM_ALL),
        name="take_step",
    )(sums, labels, *searches, *images)


def on_device(labels, basis, gains, tiles, tile_cols, tile_valid):
    labels, basis, tiles = labels[0], basis[0], tiles[0]
    rows_dev, classes = labels.shape
    row_blocks, slots, tile_size = tiles.shape[:3]
    group = lax.axis_size("blk")
    tiles = tiles.reshape(row_blocks * slots, tile_size, tile_size)
    blk, y, x, core = (lax.axis_index(a) for a in ("blk", "y", "x", "core"))
    place = jnp.stack([core, blk]).astype(jnp.int32)

    cols = tile_cols.reshape(-1)
    valid = tile_valid.reshape(-1)

    sent = shift(project(place, basis, labels, False), "core", 1)
    chip_sum = project(place, basis, labels, True) + sent
    chip_sum, later_tiles = lax.optimization_barrier((chip_sum, tiles))
    row_total, col_parts = degree_parts(later_tiles, cols, valid, row_blocks * group, slots)
    extra = rows_dev // classes
    col_parts = col_parts.reshape(group * extra, classes)
    half = chip_sum.shape[0]
    peers = lax.axis_size(PLANE)
    pieces = lax.all_to_all(chip_sum.reshape(peers, half // peers, classes), PLANE, 0, 0)
    share = jnp.sum(pieces, axis=0)
    share, col_parts = lax.optimization_barrier((share, col_parts))
    share_rows = share.shape[0]

    def with_cols(k):
        part = lax.dynamic_slice_in_dim(col_parts, ((blk + k) % group) * extra, extra)
        return jnp.concatenate([share, part], axis=0)

    joined = with_cols(0)
    for part in [shift(with_cols(k), "blk", k) for k in range(1, group)]:
        joined = joined + part
    share = joined[:share_rows]
    share = share + shift(share, "zh", 1)
    degree = 0.5 * (row_total + joined[share_rows:].reshape(rows_dev, 1))
    offset = core * half + (y * lax.axis_size("x") + x) * share_rows
    local_gain = lax.dynamic_slice_in_dim(gains, offset, share_rows)
    coeffs = (local_gain[:, None] * share).astype(BF16)
    mine = to_all(coeffs, PLANE).reshape(half, classes)
    theirs = shift(mine, "core", 1)

    searches, images, dots = [], [], []
    for chunk in range(CHUNKS):
        search, rounded, dot_rz = spread(place, labels, basis, mine, theirs, rows_dev, chunk)
        placed, pair = [], (rounded, rounded)
        for k in range(1, group):
            pair = both_ways(pair, k - 1)
            placed += [(-k, 0, pair[0]), (k, 0, pair[1])]
        image, dot_image = apply(
            cols, valid, place, tiles, degree, search, rounded, placed, slots, chunk
        )
        searches.append(search)
        images.append(image)
        dots.append(jnp.concatenate([dot_rz, dot_image], axis=0))
    sums = jnp.concatenate(dots, axis=1)
    sums = jnp.sum(to_all(sums, ("y", "x", "core")), axis=0)
    sums = to_all(sums, COLUMN)
    solution_out, residual_out = take_step(sums, labels, searches, images, rows_dev // 2)
    return solution_out[None], residual_out[None]


def solution(mesh):
    blk, sample = mesh.devices.shape
    fine = Mesh(mesh.devices.reshape(blk, 4, 4, 2, sample // 32), FINE)
    return jax.shard_map(
        on_device,
        mesh=fine,
        in_specs=(
            P(SAMPLE, "blk", None),
            P(SAMPLE, "blk", None),
            P(),
            P(SAMPLE, "blk", None, None, None),
            P(SAMPLE, "blk", None),
            P(SAMPLE, "blk", None),
        ),
        out_specs=(P(SAMPLE, "blk", None), P(SAMPLE, "blk", None)),
        check_vma=False,
    )
```

```python
import functools

import jax
import jax.numpy as jnp
from jax import lax
from jax.experimental import pallas as pl
from jax.experimental.pallas import tpu as pltpu
from jax.sharding import Mesh, PartitionSpec as P

F32 = jnp.float32
BF16 = jnp.bfloat16
FINE = ("blk", "y", "x", "zh", "core")
SAMPLE = ("y", "x", "zh", "core")
PLANE = ("y", "x")
COLUMN = ("blk", "zh")
VMEM_SOME = 32 * 1024 * 1024
VMEM_ALL = 60 * 1024 * 1024
CHUNKS = 2


def params(limit=VMEM_SOME):
    return pltpu.CompilerParams(vmem_limit_bytes=limit)


def shift(value, axis, by):
    size = lax.axis_size(axis)
    return lax.ppermute(value, axis, [(i, (i + by) % size) for i in range(size)])


def along_line(value, by, skip):
    size = lax.axis_size("blk")
    if by > 0:
        pairs = [(i, i + 1) for i in range(skip, size - 1)]
    else:
        pairs = [(i, i - 1) for i in range(1, size - skip)]
    return lax.ppermute(value, "blk", pairs)


def both_ways(pair, skip):
    return along_line(pair[0], 1, skip), along_line(pair[1], -1, skip)


def all_sum(value, axis):
    total = value
    for part in [shift(value, axis, k) for k in range(1, lax.axis_size(axis))]:
        total = total + part
    return total


def to_all(value, axes):
    copies = jnp.broadcast_to(value[None], (lax.axis_size(axes),) + value.shape)
    return lax.all_to_all(copies, axes, 0, 0)


def project_kernel(place, basis, labels, out):
    @pl.when(pl.program_id(0) == 0)
    def _():
        out[...] = jnp.zeros_like(out)

    out[...] += lax.dot_general(
        basis[...], labels[...], (((0,), (0,)), ((), ())), preferred_element_type=F32
    )


def project(place, basis, labels, own, pieces, piece):
    rows, classes = labels.shape
    half = basis.shape[1] // (2 * pieces)
    steps = 1
    part = rows // steps
    side = lambda i, p: (i, (p[0] if own else 1 - p[0]) * pieces + piece)
    return pl.pallas_call(
        project_kernel,
        grid_spec=pltpu.PrefetchScalarGridSpec(
            num_scalar_prefetch=1,
            grid=(steps,),
            in_specs=[
                pl.BlockSpec((part, half), side),
                pl.BlockSpec((part, classes), lambda i, p: (i, 0)),
            ],
            out_specs=pl.BlockSpec((half, classes), lambda i, p: (0, 0)),
        ),
        out_shape=jax.ShapeDtypeStruct((half, classes), F32),
        compiler_params=params(),
        cost_estimate=pl.CostEstimate(
            flops=2 * rows * half * classes, bytes_accessed=4 * rows * half, transcendentals=0
        ),
        name="project_own" if own else f"project_other_{piece}",
    )(place, basis, labels)


def degree_parts_kernel(cols, valid, tiles, rows_out, cols_out):
    step = pl.program_id(0)
    slots = tiles.shape[0]

    @pl.when(step == 0)
    def _():
        cols_out[...] = jnp.zeros_like(cols_out)

    total = jnp.zeros(tiles.shape[1:], F32)
    for t in range(slots):
        at = step * slots + t
        tile = tiles[t].astype(F32) * valid[at].astype(F32)
        total = total + tile
        cols_out[pl.ds(cols[at], 1), :] += jnp.sum(tile, axis=0, keepdims=True)
    rows_out[...] = jnp.sum(total, axis=1, keepdims=True)


def degree_parts(tiles, cols, valid, col_blocks, slots):
    count, size, _ = tiles.shape
    steps = count // slots
    return pl.pallas_call(
        degree_parts_kernel,
        grid_spec=pltpu.PrefetchScalarGridSpec(
            num_scalar_prefetch=2,
            grid=(steps,),
            in_specs=[pl.BlockSpec((slots, size, size), lambda i, c, v: (i, 0, 0))],
            out_specs=[
                pl.BlockSpec((size, 1), lambda i, c, v: (i, 0)),
                pl.BlockSpec((col_blocks, size), lambda i, c, v: (0, 0)),
            ],
        ),
        out_shape=[
            jax.ShapeDtypeStruct((steps * size, 1), F32),
            jax.ShapeDtypeStruct((col_blocks, size), F32),
        ],
        cost_estimate=pl.CostEstimate(
            flops=4 * tiles.size, bytes_accessed=2 * tiles.size, transcendentals=0
        ),
        name="degree_parts",
    )(cols, valid, tiles)


def spread_of(basis_own, basis_other, mine, theirs):
    return jnp.dot(basis_own[...], mine[...], preferred_element_type=F32) + jnp.dot(
        basis_other[...], theirs[...], preferred_element_type=F32
    )


def moves(sources, targets, sems, size, count):
    return [
        pltpu.make_async_copy(
            sources.at[pl.ds(k * size, size), :], targets.at[pl.ds(k * size, size), :], sems.at[k]
        )
        for k in range(count)
    ]


def start_at(copies, step):
    for k, copy in enumerate(copies):
        pl.when(step == k)(copy.start)


def spread_kernel(
    place, labels, own, other, mine, theirs, search, rounded, dots, v_search, sems
):
    step, steps = pl.program_id(0), pl.num_programs(0)
    size = labels.shape[0]

    @pl.when(step == 0)
    def _():
        dots[...] = jnp.zeros_like(dots)

    residual = labels[...].astype(F32)
    value = residual + spread_of(own, other, mine, theirs)
    rounded[...] = value.astype(BF16)
    v_search[pl.ds(pl.multiple_of(step * size, size), size), :] = value
    dots[...] += jnp.sum(residual * value, axis=0, keepdims=True)
    stores = moves(v_search, search, sems, size, v_search.shape[0] // size)
    start_at(stores, step)

    @pl.when(step == steps - 1)
    def _():
        for copy in stores:
            copy.wait()


def spread(place, labels, basis, mine, theirs, part, chunk):
    rows, classes = labels.shape
    half = mine.shape[0]
    width = classes // CHUNKS
    block = pl.BlockSpec((part, width), lambda i, p: (i, 0))
    columns = pl.BlockSpec((half, width), lambda i, p: (0, chunk))
    return pl.pallas_call(
        spread_kernel,
        grid_spec=pltpu.PrefetchScalarGridSpec(
            num_scalar_prefetch=1,
            grid=(rows // part,),
            in_specs=[
                pl.BlockSpec((part, width), lambda i, p: (i, chunk)),
                pl.BlockSpec((part, half), lambda i, p: (i, p[0])),
                pl.BlockSpec((part, half), lambda i, p: (i, 1 - p[0])),
                columns,
                columns,
            ],
            out_specs=[
                pl.BlockSpec(memory_space=pltpu.HBM),
                block,
                pl.BlockSpec((1, width), lambda i, p: (0, 0)),
            ],
            scratch_shapes=[
                pltpu.VMEM((rows, width), F32),
                pltpu.SemaphoreType.DMA((rows // part,)),
            ],
        ),
        out_shape=[
            jax.ShapeDtypeStruct((rows, width), F32),
            jax.ShapeDtypeStruct((rows, width), BF16),
            jax.ShapeDtypeStruct((1, width), F32),
        ],
        compiler_params=params(),
        cost_estimate=pl.CostEstimate(
            flops=4 * rows * half * width, bytes_accessed=16 * rows * width, transcendentals=0
        ),
        name=f"spread_{chunk}",
    )(place, labels, basis, basis, mine, theirs)


def apply_kernel(places, cols, valid, place, tiles, degree, search, own, *rest):
    pieces, (image, dots, panel, v_search, v_image, sems, in_sems, out_sems) = rest[:-8], rest[-8:]
    count, size, _ = tiles.shape
    rows = own.shape[0]
    blocks = rows // size
    slots = count // blocks
    me = place[1]
    last = panel.shape[0] // rows - 1

    def copies(act):
        for k, (offset, start) in enumerate(places):
            owner = me + offset

            @pl.when(jnp.logical_and(owner >= 0, owner <= last))
            def _(k=k, owner=owner, start=start):
                at = pl.multiple_of(owner * rows + start, size)
                target = panel.at[pl.ds(at, pieces[k].shape[0]), :]
                act(pltpu.make_async_copy(pieces[k], target, sems.at[k]))

    copies(lambda copy: copy.start())
    loads = moves(search, v_search, in_sems, size, blocks)
    stores = moves(v_image, image, out_sems, size, blocks)
    for copy in loads:
        copy.start()
    panel[pl.ds(pl.multiple_of(me * rows, size), rows), :] = own[...]
    copies(lambda copy: copy.wait())
    sums = jnp.zeros(dots.shape, F32)
    for b in range(blocks):
        loads[b].wait()
        here = pl.ds(b * size, size)
        value = v_search[here, :]
        total = value + 0.5 * (degree[here, :] * value)
        for t in range(b * slots, (b + 1) * slots):
            block = panel[pl.ds(pl.multiple_of(cols[t] * size, size), size), :]
            product = jnp.dot(tiles[t], block, preferred_element_type=F32)
            total = total - (0.5 * valid[t].astype(F32)) * product
        v_image[here, :] = total
        stores[b].start()
        sums = sums + jnp.sum(value * total, axis=0, keepdims=True)
    dots[...] = sums
    for copy in stores:
        copy.wait()


def apply(cols, valid, place, tiles, degree, search, own, placed, slots, chunk):
    rows, classes = search.shape
    count, size, _ = tiles.shape
    in_hbm = pl.BlockSpec(memory_space=pltpu.HBM)
    places = tuple(item[:2] for item in placed)
    pieces = [item[2] for item in placed]
    return pl.pallas_call(
        functools.partial(apply_kernel, places),
        grid_spec=pltpu.PrefetchScalarGridSpec(
            num_scalar_prefetch=3,
            grid=(1,),
            in_specs=[
                pl.BlockSpec(tiles.shape, lambda i, c, v, p: (0, 0, 0)),
                pl.BlockSpec((rows, 1), lambda i, c, v, p: (0, 0)),
                in_hbm,
                pl.BlockSpec((rows, classes), lambda i, c, v, p: (0, 0)),
            ]
            + [pl.BlockSpec(memory_space=pl.ANY)] * len(pieces),
            out_specs=[in_hbm, pl.BlockSpec((1, classes), lambda i, c, v, p: (0, 0))],
            scratch_shapes=[
                pltpu.VMEM((lax.axis_size("blk") * rows, classes), BF16),
                pltpu.VMEM((rows, classes), F32),
                pltpu.VMEM((rows, classes), F32),
                pltpu.SemaphoreType.DMA((len(pieces),)),
                pltpu.SemaphoreType.DMA((count // slots,)),
                pltpu.SemaphoreType.DMA((count // slots,)),
            ],
        ),
        out_shape=[
            jax.ShapeDtypeStruct((rows, classes), F32),
            jax.ShapeDtypeStruct((1, classes), F32),
        ],
        compiler_params=params(),
        cost_estimate=pl.CostEstimate(
            flops=2 * count * size * size * classes,
            bytes_accessed=20 * rows * classes,
            transcendentals=0,
        ),
        name=f"apply_{chunk}",
    )(cols, valid, place, tiles, degree, search, own, *pieces)


def step_kernel(sums, labels, *refs):
    searches, images = refs[:CHUNKS], refs[CHUNKS : 2 * CHUNKS]
    solution_out, residual_out = refs[2 * CHUNKS :]
    total = jnp.sum(sums[...], axis=0)
    size = total[0:1, :] / total[1:2, :]
    width = searches[0].shape[1]
    for k in range(CHUNKS):
        at = slice(k * width, (k + 1) * width)
        solution_out[:, at] = size[:, at] * searches[k][...]
        residual_out[:, at] = labels[:, at].astype(F32) - size[:, at] * images[k][...]


def take_step(sums, labels, searches, images, part):
    rows, classes = labels.shape
    block = pl.BlockSpec((part, classes), lambda i: (i, 0))
    piece = pl.BlockSpec((part, classes // CHUNKS), lambda i: (i, 0))
    return pl.pallas_call(
        step_kernel,
        grid=(rows // part,),
        in_specs=[pl.BlockSpec(sums.shape, lambda i: (0, 0, 0)), block] + [piece] * 2 * CHUNKS,
        out_specs=[block, block],
        out_shape=[jax.ShapeDtypeStruct((rows, classes), F32)] * 2,
        compiler_params=params(VMEM_ALL),
        name="take_step",
    )(sums, labels, *searches, *images)


def on_device(labels, basis, gains, tiles, tile_cols, tile_valid):
    labels, basis, tiles = labels[0], basis[0], tiles[0]
    rows_dev, classes = labels.shape
    row_blocks, slots, tile_size = tiles.shape[:3]
    group = lax.axis_size("blk")
    tiles = tiles.reshape(row_blocks * slots, tile_size, tile_size)
    blk, y, x, core = (lax.axis_index(a) for a in ("blk", "y", "x", "core"))
    place = jnp.stack([core, blk]).astype(jnp.int32)

    cols = tile_cols.reshape(-1)
    valid = tile_valid.reshape(-1)

    sent = [shift(project(place, basis, labels, False, 2, k), "core", 1) for k in range(2)]
    chip_sum = project(place, basis, labels, True, 1, 0) + jnp.concatenate(sent, axis=0)
    chip_sum, later_tiles = lax.optimization_barrier((chip_sum, tiles))
    row_total, col_parts = degree_parts(later_tiles, cols, valid, row_blocks * group, slots)
    extra = rows_dev // classes
    col_parts = col_parts.reshape(group * extra, classes)
    half = chip_sum.shape[0]
    peers = lax.axis_size(PLANE)
    pieces = lax.all_to_all(chip_sum.reshape(peers, half // peers, classes), PLANE, 0, 0)
    share = jnp.sum(pieces, axis=0)
    share, col_parts = lax.optimization_barrier((share, col_parts))
    share_rows = share.shape[0]

    def with_cols(k):
        part = lax.dynamic_slice_in_dim(col_parts, ((blk + k) % group) * extra, extra)
        return jnp.concatenate([share, part], axis=0)

    joined = with_cols(0)
    for part in [shift(with_cols(k), "blk", k) for k in range(1, group)]:
        joined = joined + part
    share = joined[:share_rows]
    share = share + shift(share, "zh", 1)
    degree = 0.5 * (row_total + joined[share_rows:].reshape(rows_dev, 1))
    offset = core * half + (y * lax.axis_size("x") + x) * share_rows
    local_gain = lax.dynamic_slice_in_dim(gains, offset, share_rows)
    coeffs = (local_gain[:, None] * share).astype(BF16)
    mine = to_all(coeffs, PLANE).reshape(half, classes)
    theirs = shift(mine, "core", 1)

    searches, images, dots = [], [], []
    for chunk in range(CHUNKS):
        search, rounded, dot_rz = spread(place, labels, basis, mine, theirs, rows_dev, chunk)
        placed, pair = [], (rounded, rounded)
        for k in range(1, group):
            pair = both_ways(pair, k - 1)
            placed += [(-k, 0, pair[0]), (k, 0, pair[1])]
        image, dot_image = apply(
            cols, valid, place, tiles, degree, search, rounded, placed, slots, chunk
        )
        searches.append(search)
        images.append(image)
        dots.append(jnp.concatenate([dot_rz, dot_image], axis=0))
    sums = jnp.concatenate(dots, axis=1)
    sums = jnp.sum(to_all(sums, ("y", "x", "core")), axis=0)
    sums = to_all(sums, COLUMN)
    solution_out, residual_out = take_step(sums, labels, searches, images, rows_dev // 2)
    return solution_out[None], residual_out[None]


def solution(mesh):
    blk, sample = mesh.devices.shape
    fine = Mesh(mesh.devices.reshape(blk, 4, 4, 2, sample // 32), FINE)
    return jax.shard_map(
        on_device,
        mesh=fine,
        in_specs=(
            P(SAMPLE, "blk", None),
            P(SAMPLE, "blk", None),
            P(),
            P(SAMPLE, "blk", None, None, None),
            P(SAMPLE, "blk", None),
            P(SAMPLE, "blk", None),
        ),
        out_specs=(P(SAMPLE, "blk", None), P(SAMPLE, "blk", None)),
        check_vma=False,
    )
```
